128 devices in a mesh: row: 8 (over z, x_lo), col: 16 (over y, x_hi, core).
Axes of the slice: x: 4 (x_hi: 2, x_lo: 2; x = x_hi * 2 + x_lo), y: 4, z: 4, core: 2. Of those that a mesh axis runs over, the one named last changes fastest.
Arguments:
- edge_left: bfloat16 [8, 2048, 4096], P(None, 'row', 'col'), may hold values from -6 to 6
- site_left: bfloat16 [8, 4096, 2048], P(None, 'col'), may hold values from -0.09375 to 0.09375
- edge_right: bfloat16 [8, 2048, 4096], P(None, None, 'row'), may hold values from -6 to 6
- site_right: bfloat16 [8, 4096, 2048], P(None, 'row', 'col'), may hold values from -0.09375 to 0.09375
- sector_sizes: int32 [8], replicated, may hold values from 1 to 2048, 9216 in all
Outputs:
- half_system: bfloat16 [8, 2048, 2048], P(None, 'row', 'col')
The draws below stay inside these ranges and needn't reach their ends.
Inputs may be any that keep to these rules, and one draw needn't show every extreme that they name: `sector_sizes`: every sector size is at least 1, one sector has exactly 2048, and the sizes sum to 9216.
All inputs are finite; a program needn't handle non-finite values.
Results may differ from the reference program's by a relative error of at most 0.025.
Values may be sent and summed in bfloat16 or wider, within the bound.
No kernel may reach another device: no remote copies, remote signals or barrier semaphores. Data moves between devices by JAX's collectives and lax.ppermute only.
A program may use at most 128 MiB of HBM per device.

```python
import math
import jax
import jax.numpy as jnp
import numpy as np
from jax import lax

BLK = 2048
KB = 4096
SECTORS = 8
N_ROW = 8
N_COL = 16


def level_of(key, dims, pieces, low, top_value):
    def one(axis_at, shards_of):
        steps = jax.random.uniform(jax.random.fold_in(jax.random.fold_in(key, 6), axis_at), (shards_of,), jnp.float32, low / len(pieces), top_value / len(pieces))
        return jnp.repeat(jnp.exp(steps), dims[axis_at] // shards_of).reshape((-1,) + (1,) * (len(dims) - axis_at - 1))

    level = one(*pieces[0])
    for cut in pieces[1:]:
        level = level * one(*cut)
    return level


def split_up(count, total, reach, lean):
    portions = [(1 << 20) // math.isqrt(standing ** lean) + 1 for standing in range(2, count + 1)]
    rest, counts = total - reach - (count - 1), [1] * (count - 1)
    while rest > 0:
        free = [i for i in range(count - 1) if counts[i] < reach]
        pool, budget = sum([portions[i] for i in free]), rest
        for i in free:
            addition = min(reach - counts[i], max(1, budget * portions[i] // pool), rest)
            counts[i] = counts[i] + addition
            rest = rest - addition
    return np.array([reach] + counts)


def ragged_sizes(stream_key, amount, total, most, slope):
    if amount == 2:
        one = jax.random.randint(stream_key, (), max(1, total - most), min(most, total - 1) + 1)
        return jnp.stack([one, total - one])
    tallies = jnp.asarray(split_up(amount, total, most, slope), jnp.int32)
    twos = (amount - 1) // 2
    source_of, sink = tallies[1:1 + 2 * twos:2], tallies[2:2 + 2 * twos:2]
    slack = jnp.minimum(source_of - 1, most - sink)
    passed = jax.random.randint(jax.random.fold_in(stream_key, 1), (twos,), 0, 1 << 20) % (slack + 1)
    tallies = tallies.at[1:1 + 2 * twos:2].set(source_of - passed).at[2:2 + 2 * twos:2].set(sink + passed)
    return tallies[jax.random.permutation(jax.random.fold_in(stream_key, 2), amount)]


def centred(own_key, shape, scale, most, cuts=(), kind=jnp.bfloat16):
    result = scale * jax.random.normal(own_key, shape, jnp.float32)
    if cuts:
        result = result * level_of(own_key, shape, cuts, -0.22, 0.18)
    return jnp.clip(result, -most, most).astype(kind)


def setup_inputs(seed: int = 0) -> dict:
    arg_keys = jax.random.split(jax.random.key(seed), 6)
    edge_left = centred(arg_keys[0], (SECTORS, BLK, KB), 1.0, 6.0, ((1, 8), (2, 16)))
    site_left = centred(arg_keys[1], (SECTORS, KB, BLK), KB ** -0.5, 0.09375, ((1, 16),))
    edge_right = centred(arg_keys[2], (SECTORS, BLK, KB), 1.0, 6.0, ((2, 8),))
    site_right = centred(arg_keys[3], (SECTORS, KB, BLK), KB ** -0.5, 0.09375, ((1, 8), (2, 16)))
    sector_sizes = ragged_sizes(arg_keys[4], SECTORS, BLK + (SECTORS - 1) * (BLK // 2), BLK, 2).astype(jnp.int32)
    return dict(edge_left=edge_left, site_left=site_left, edge_right=edge_right, site_right=site_right, sector_sizes=sector_sizes)


def live_mask(sector_sizes):
    index_line = jnp.arange(BLK, dtype=jnp.int32)
    inside = index_line[None, :] < sector_sizes[:, None]
    return inside[:, :, None] & inside[:, None, :]


def corner(edge_part, site_part, live, groups):
    width = KB // groups
    edge_groups = edge_part.reshape(SECTORS, BLK, groups, width).transpose(2, 0, 1, 3)
    site_groups = site_part.reshape(SECTORS, groups, width, BLK).transpose(1, 0, 2, 3)

    def add_group(total, pair):
        edge_piece, site_piece = pair
        term = jnp.einsum('sik,skj->sij', edge_piece.astype(jnp.float32), site_piece.astype(jnp.float32))
        rounded = lax.optimization_barrier(term.astype(jnp.bfloat16))
        return total + rounded.astype(jnp.float32), None

    initial = jnp.zeros((SECTORS, BLK, BLK), jnp.float32)
    summed, _ = lax.scan(add_group, initial, (edge_groups, site_groups))
    return jnp.where(live, summed, jnp.float32(0.0)).astype(jnp.bfloat16)


def reference(edge_left, site_left, edge_right, site_right, sector_sizes):
    live = live_mask(sector_sizes)
    corner_one = corner(edge_left, site_left, live, N_COL)
    corner_two = corner(edge_right, site_right, live, N_ROW)
    product = jnp.einsum('sik,skj->sij', corner_one.astype(jnp.float32), corner_two.astype(jnp.float32))
    return (product * jnp.float32(BLK ** -0.5)).astype(jnp.bfloat16)
```

```python
import jax
import jax.numpy as jnp
from jax import lax
from jax.experimental import pallas as pl
from jax.experimental.pallas import tpu as pltpu
from jax.sharding import Mesh
from jax.sharding import PartitionSpec as P

WIDTH = 128
SLOTS = 80
HALF = SLOTS // 2
Z, XL, Y, XH, CORE = 4, 2, 4, 2, 2
ONE = HALF // (Y * XH)
TWO = SLOTS // (Z * XL)


def slot_table(sector_sizes):
    sectors = sector_sizes.shape[0]
    blocks = (sector_sizes + (WIDTH - 1)) // WIDTH
    line = jnp.arange(sectors, dtype=jnp.int32)
    ends = jnp.sum(jnp.where(line[None, :] <= line[:, None], blocks[None, :], 0), axis=1)
    firsts = ends - blocks
    slot = jnp.arange(SLOTS, dtype=jnp.int32)
    past = slot[:, None] >= ends[None, :]
    inside = (slot[:, None] >= firsts[None, :]) & ~past
    sector = jnp.minimum(jnp.sum(past.astype(jnp.int32), axis=1), sectors - 1)
    block = jnp.sum(jnp.where(inside, slot[:, None] - firsts[None, :], 0), axis=1)
    limit = jnp.sum(jnp.where(inside, sector_sizes[None, :], 0), axis=1)
    return firsts, ends, sector, block, limit


def masked(values, row_limit, col_limit):
    rows = lax.broadcasted_iota(jnp.int32, values.shape, 0)
    cols = lax.broadcasted_iota(jnp.int32, values.shape, 1)
    return jnp.where((rows < row_limit) & (cols < col_limit), values, jnp.float32(0.0))


def left_kernel(add, where_ref, sector_ref, block_ref, limit_ref, edge_ref, site_ref, *rest):
    if add:
        other_ref, out_ref, site_buf, sems = rest
    else:
        out_ref, site_buf, sems = rest
    first_slot = where_ref[0]
    row_first = where_ref[1]

    def fetch(q):
        p = first_slot + q
        return pltpu.make_async_copy(
            site_ref.at[sector_ref[p], :, pl.ds(pl.multiple_of(block_ref[p] * WIDTH, WIDTH), WIDTH)],
            site_buf.at[q],
            sems.at[q],
        )

    @pl.loop(0, HALF)
    def _(q):
        fetch(q).start()

    @pl.loop(0, HALF // 4)
    def _(group):
        for k in range(4):
            fetch(group * 4 + k).wait()
        for k in range(4):
            q = group * 4 + k
            p = first_slot + q
            limit = limit_ref[p]
            term = jnp.dot(edge_ref[sector_ref[p]], site_buf[q], preferred_element_type=jnp.float32)
            if add:
                term = term + other_ref[q].astype(jnp.float32)
            out_ref[q] = masked(term, limit - row_first, limit - block_ref[p] * WIDTH).astype(jnp.bfloat16)


def left_terms(add, first_slot, row_first, table, edge, site, *other):
    rows, depth = edge.shape[1], edge.shape[2]
    vmem = pl.BlockSpec(memory_space=pltpu.VMEM)
    spec = pltpu.PrefetchScalarGridSpec(
        num_scalar_prefetch=4,
        grid=(1,),
        in_specs=[vmem, pl.BlockSpec(memory_space=pl.ANY)] + [vmem] * len(other),
        out_specs=vmem,
        scratch_shapes=[
            pltpu.VMEM((HALF, depth, WIDTH), jnp.bfloat16),
            pltpu.SemaphoreType.DMA((HALF,)),
        ],
    )
    return pl.pallas_call(
        lambda *refs: left_kernel(add, *refs),
        out_shape=jax.ShapeDtypeStruct((HALF, rows, WIDTH), jnp.bfloat16),
        grid_spec=spec,
        compiler_params=pltpu.CompilerParams(vmem_limit_bytes=32 * 2**20),
        cost_estimate=pl.CostEstimate(
            flops=2 * HALF * rows * depth * WIDTH, bytes_accessed=10 * 2**20, transcendentals=0
        ),
        name="left_add" if add else "left",
    )(jnp.stack([first_slot, row_first]).astype(jnp.int32), *table, edge, site, *other)


def right_kernel(where_ref, sector_ref, block_ref, limit_ref, edge_ref, site_ref, *rest):
    outs, (edge_buf, sems) = rest[:Z], rest[Z:]
    z = where_ref[0]
    x = where_ref[1]
    col_first = where_ref[2]
    per_z = XL * TWO

    def slot(step, q):
        return lax.rem(z + step, Z) * per_z + jnp.where(q < TWO, x * TWO + q, (1 - x) * TWO + q - TWO)

    def fetch(step, q):
        p = slot(step, q)
        at = step * per_z + q
        return pltpu.make_async_copy(
            edge_ref.at[sector_ref[p], pl.ds(pl.multiple_of(block_ref[p] * WIDTH, WIDTH), WIDTH), :],
            edge_buf.at[at],
            sems.at[at],
        )

    order = (2, 1, 3, 0)
    for step in order:

        @pl.loop(0, per_z)
        def _(q):
            fetch(step, q).start()

    for step in order:

        @pl.loop(0, per_z // 4)
        def _(group):
            for k in range(4):
                fetch(step, group * 4 + k).wait()
            for k in range(4):
                q = group * 4 + k
                p = slot(step, q)
                limit = limit_ref[p]
                term = jnp.dot(
                    edge_buf[step * per_z + q], site_ref[sector_ref[p]], preferred_element_type=jnp.float32
                )
                outs[step][q] = masked(term, limit - block_ref[p] * WIDTH, limit - col_first).astype(
                    jnp.bfloat16
                )


def right_terms(z, x, col_first, table, edge, site):
    depth, cols = site.shape[1], site.shape[2]
    vmem = pl.BlockSpec(memory_space=pltpu.VMEM)
    spec = pltpu.PrefetchScalarGridSpec(
        num_scalar_prefetch=4,
        grid=(1,),
        in_specs=[pl.BlockSpec(memory_space=pl.ANY), vmem],
        out_specs=[vmem] * Z,
        scratch_shapes=[
            pltpu.VMEM((SLOTS, WIDTH, depth), jnp.bfloat16),
            pltpu.SemaphoreType.DMA((SLOTS,)),
        ],
    )
    return pl.pallas_call(
        right_kernel,
        out_shape=[jax.ShapeDtypeStruct((XL * TWO, WIDTH, cols), jnp.bfloat16)] * Z,
        grid_spec=spec,
        compiler_params=pltpu.CompilerParams(vmem_limit_bytes=32 * 2**20),
        cost_estimate=pl.CostEstimate(
            flops=2 * SLOTS * WIDTH * depth * cols, bytes_accessed=16 * 2**20, transcendentals=0
        ),
        name="right",
    )(jnp.stack([z, x, col_first]).astype(jnp.int32), *table, edge, site)


def product_kernel(scale, where_ref, first_ref, end_ref, own_ref, other_ref, *rest):
    rights = rest[:Z]
    out_ref, one_buf, two_buf, sems = rest[Z:]
    core, z, x = where_ref[0], where_ref[1], where_ref[2]
    per_z = XL * TWO
    copies = [
        pltpu.make_async_copy(own_ref, one_buf.at[pl.ds(core * HALF, HALF)], sems.at[0]),
        pltpu.make_async_copy(other_ref, one_buf.at[pl.ds((1 - core) * HALF, HALF)], sems.at[1]),
    ]
    for step in range(Z):
        base = lax.rem(z + Z - step, Z) * per_z
        for k in range(XL):
            at = base + (x if k == 0 else 1 - x) * TWO
            copies.append(
                pltpu.make_async_copy(
                    rights[step].at[pl.ds(k * TWO, TWO)], two_buf.at[pl.ds(at, TWO)], sems.at[2 + step * XL + k]
                )
            )
    for copy in copies:
        copy.start()
    for copy in copies:
        copy.wait()

    @pl.loop(0, out_ref.shape[0])
    def _(s):
        def add(p, total):
            return total + jnp.dot(one_buf[p], two_buf[p], preferred_element_type=jnp.float32)

        total = lax.fori_loop(first_ref[s], end_ref[s], add, jnp.zeros(out_ref.shape[1:], jnp.float32))
        out_ref[s] = (total * jnp.float32(scale)).astype(jnp.bfloat16)


def product(scale, where, firsts, ends, own, other, rights):
    rows, cols, sectors = own.shape[1], rights[0].shape[2], firsts.shape[0]
    vmem = pl.BlockSpec(memory_space=pltpu.VMEM)
    anywhere = pl.BlockSpec(memory_space=pl.ANY)
    spec = pltpu.PrefetchScalarGridSpec(
        num_scalar_prefetch=3,
        grid=(1,),
        in_specs=[anywhere] * (2 + Z),
        out_specs=vmem,
        scratch_shapes=[
            pltpu.VMEM((SLOTS, rows, WIDTH), jnp.bfloat16),
            pltpu.VMEM((SLOTS, WIDTH, cols), jnp.bfloat16),
            pltpu.SemaphoreType.DMA((2 + Z * XL,)),
        ],
    )
    return pl.pallas_call(
        lambda *refs: product_kernel(scale, *refs),
        out_shape=jax.ShapeDtypeStruct((sectors, rows, cols), jnp.bfloat16),
        grid_spec=spec,
        compiler_params=pltpu.CompilerParams(vmem_limit_bytes=32 * 2**20),
        cost_estimate=pl.CostEstimate(
            flops=2 * SLOTS * rows * WIDTH * cols, bytes_accessed=9 * 2**20, transcendentals=0
        ),
        name="product",
    )(where, firsts, ends, own, other, *rights)


def shift(array, axis, size, step):
    return lax.ppermute(array, axis, [(i, (i + step) % size) for i in range(size)])


def on_device(edge_left, site_left, edge_right, site_right, sector_sizes):
    order = site_left.shape[2]
    rows, cols = edge_left.shape[1], site_right.shape[2]
    z, xl, y, xh, core = (lax.axis_index(a) for a in ("z", "xl", "y", "xh", "core"))
    row_first = (z * XL + xl) * rows
    col_first = ((y * XH + xh) * CORE + core) * cols
    firsts, ends, *table = slot_table(sector_sizes)
    f32 = lambda a: a.astype(jnp.float32)

    for_other = left_terms(False, (1 - core) * HALF, row_first, table, edge_left, site_left)
    from_other = shift(for_other, "core", CORE, 1)
    to = right_terms(z, xl, col_first, table, edge_right, site_right)
    came = [shift(to[step], "z", Z, step) for step in range(1, Z)]
    chip_sum = left_terms(True, core * HALF, row_first, table, edge_left, site_left, from_other)
    spread = lax.all_to_all(chip_sum, ("y", "xh"), 0, 0, tiled=True)

    right_sum = (f32(to[0]) + f32(came[0]) + f32(came[1]) + f32(came[2])).astype(jnp.bfloat16)
    right_x = shift(right_sum[TWO:], "xl", XL, 1)
    right_own = (f32(right_sum[:TWO]) + f32(right_x)).astype(jnp.bfloat16)
    left_own = jnp.sum(f32(spread.reshape((Y * XH, ONE, rows, WIDTH))), axis=0).astype(jnp.bfloat16)

    right_pair = jnp.concatenate([right_own, shift(right_own, "xl", XL, 1)], axis=0)
    rights = [right_pair] + [shift(right_pair, "z", Z, step) for step in range(1, Z)]
    copies = jnp.broadcast_to(left_own[None], (Y * XH, ONE, rows, WIDTH)).reshape(HALF, rows, WIDTH)
    left_half = lax.all_to_all(copies, ("y", "xh"), 0, 0, tiled=True)
    left_other = shift(left_half, "core", CORE, 1)
    where = jnp.stack([core, z, xl]).astype(jnp.int32)
    return product(order ** (-0.5), where, firsts, ends, left_half, left_other, rights)


def solution(mesh):
    split = Mesh(mesh.devices.reshape(Z, XL, Y, XH, CORE), ("z", "xl", "y", "xh", "core"))
    row, col = ("z", "xl"), ("y", "xh", "core")
    placed = (P(None, row, col), P(None, col, None), P(None, None, row), P(None, row, col), P())
    return jax.shard_map(
        on_device, mesh=split, in_specs=placed, out_specs=P(None, row, col), check_vma=False
    )
```

```python
import jax
import jax.numpy as jnp
from jax import lax
from jax.experimental import pallas as pl
from jax.experimental.pallas import tpu as pltpu
from jax.sharding import Mesh
from jax.sharding import PartitionSpec as P

WIDTH = 128
PART = 40
CHUNK = 4
Z, XL, Y, XH, CORE = 4, 2, 4, 2, 2
HALF = PART // CORE
ONE = HALF // Y
TWO = PART // Z
HBM = pl.BlockSpec(memory_space=pltpu.HBM)
VMEM = pl.BlockSpec(memory_space=pltpu.VMEM)
SMEM = pl.BlockSpec(memory_space=pltpu.SMEM)
PARAMS = pltpu.CompilerParams(vmem_limit_bytes=60 * 2**20)


def packed(size_ref, lo, hi):
    first, chunk, plan = 0, 0, []
    for s in range(size_ref.shape[0]):
        blocks = (size_ref[s] + (WIDTH - 1)) // WIDTH
        begin, end = jnp.clip(lo - first, 0, blocks), jnp.clip(hi - first, 0, blocks)
        chunks = (end - begin + (CHUNK - 1)) // CHUNK
        plan.append((first, begin, end, chunk, chunks))
        first, chunk = first + blocks, chunk + chunks
    return plan, first


def most_chunks(slots, sectors):
    return (slots + sectors * (CHUNK - 1)) // CHUNK


def left_kernel(add, at_ref, size_ref, edge_ref, site_ref, *rest):
    if add:
        other_ref, out_ref, edge_buf, site_buf, edge_sem, site_sem, other_buf, other_sem = rest
        other = pltpu.make_async_copy(other_ref, other_buf, other_sem)
    else:
        out_ref, edge_buf, site_buf, edge_sem, site_sem = rest
    lo = at_ref[0]
    plan, used = packed(size_ref, lo, lo + HALF)
    last = site_ref.shape[2] // WIDTH - CHUNK

    def block_of(s, c):
        return jnp.minimum(plan[s][1] + c * CHUNK, last)

    def fetch(s, c):
        at = plan[s][3] + c
        columns = pl.ds(pl.multiple_of(block_of(s, c) * WIDTH, WIDTH), CHUNK * WIDTH)
        return pltpu.make_async_copy(site_ref.at[s, :, columns], site_buf.at[at], site_sem.at[at])

    edges = [pltpu.make_async_copy(edge_ref.at[s], edge_buf.at[s], edge_sem.at[s]) for s in range(len(plan))]
    for s in range(len(plan)):
        edges[s].start()

        @pl.loop(0, plan[s][4])
        def _(c):
            fetch(s, c).start()

    if add:
        other.start()

    @pl.loop(jnp.clip(used - lo, 0, HALF), HALF)
    def _(q):
        out_ref[q] = jnp.zeros(out_ref.shape[1:], out_ref.dtype)

    if add:
        other.wait()
    for s in range(len(plan)):
        first, begin, end, chunk, chunks = plan[s]
        edges[s].wait()

        @pl.loop(0, chunks)
        def _(c):
            fetch(s, c).wait()
            block = block_of(s, c)
            term = jnp.dot(edge_buf[s], site_buf[chunk + c], preferred_element_type=jnp.float32)
            for k in range(CHUNK):

                @pl.when((block + k >= begin) & (block + k < end))
                def _():
                    q = first + block + k - lo
                    part = term[:, k * WIDTH : (k + 1) * WIDTH]
                    if add:
                        part = part + other_buf[q].astype(jnp.float32)
                    out_ref[q] = part.astype(out_ref.dtype)


def left_terms(first_slot, sizes, edge, site, *other):
    sectors, rows, depth = edge.shape
    most = most_chunks(HALF, sectors)
    add = bool(other)
    slots = (HALF, rows, WIDTH)
    return pl.pallas_call(
        lambda *refs: left_kernel(add, *refs),
        out_shape=jax.ShapeDtypeStruct(slots, jnp.bfloat16),
        in_specs=[SMEM, SMEM, HBM, HBM] + [HBM] * add,
        out_specs=VMEM,
        scratch_shapes=[
            pltpu.VMEM((sectors, rows, depth), jnp.bfloat16),
            pltpu.VMEM((most, depth, CHUNK * WIDTH), jnp.bfloat16),
            pltpu.SemaphoreType.DMA((sectors,)),
            pltpu.SemaphoreType.DMA((most,)),
        ]
        + [pltpu.VMEM(slots, jnp.bfloat16), pltpu.SemaphoreType.DMA] * add,
        compiler_params=PARAMS,
        cost_estimate=pl.CostEstimate(
            flops=2 * HALF * rows * depth * WIDTH, bytes_accessed=6 * 2**20, transcendentals=0
        ),
        name="left_add" if add else "left",
    )(first_slot.reshape(1).astype(jnp.int32), sizes, edge, site, *other)


def right_kernel(at_ref, size_ref, edge_ref, site_ref, *rest):
    outs, (site_buf, edge_buf, term_buf, site_sem, edge_sem) = rest[:Z], rest[Z:]
    lo, z = at_ref[0], at_ref[1]
    plan, _ = packed(size_ref, lo, lo + PART)
    last = edge_ref.shape[1] // WIDTH - CHUNK

    def block_of(s, c):
        return jnp.minimum(plan[s][1] + c * CHUNK, last)

    def fetch(s, c):
        at = plan[s][3] + c
        rows = pl.ds(pl.multiple_of(block_of(s, c) * WIDTH, WIDTH), CHUNK * WIDTH)
        return pltpu.make_async_copy(edge_ref.at[s, rows, :], edge_buf.at[at], edge_sem.at[at])

    sites = [pltpu.make_async_copy(site_ref.at[s], site_buf.at[s], site_sem.at[s]) for s in range(len(plan))]
    for s in range(len(plan)):
        sites[s].start()

        @pl.loop(0, plan[s][4])
        def _(c):
            fetch(s, c).start()

    for s in range(len(plan)):
        first, _, _, chunk, chunks = plan[s]
        sites[s].wait()

        @pl.loop(0, chunks)
        def _(c):
            fetch(s, c).wait()
            term = jnp.dot(edge_buf[chunk + c], site_buf[s], preferred_element_type=jnp.float32)
            q = first + block_of(s, c) - lo + CHUNK
            term_buf[pl.ds(q, CHUNK)] = term.astype(jnp.bfloat16).reshape(CHUNK, WIDTH, term.shape[1])

    for step in range(Z):
        base = lax.rem(z + step, Z) * TWO + CHUNK
        for k in range(0, TWO, 2):
            outs[step][k : k + 2] = term_buf[pl.ds(base + k, 2)]


def right_terms(first_slot, z, sizes, edge, site):
    sectors, depth, cols = site.shape
    most = most_chunks(PART, sectors)
    return pl.pallas_call(
        right_kernel,
        out_shape=[jax.ShapeDtypeStruct((TWO, WIDTH, cols), jnp.bfloat16)] * Z,
        in_specs=[SMEM, SMEM, HBM, HBM],
        out_specs=[VMEM] * Z,
        scratch_shapes=[
            pltpu.VMEM((sectors, depth, cols), jnp.bfloat16),
            pltpu.VMEM((most, CHUNK * WIDTH, depth), jnp.bfloat16),
            pltpu.VMEM((PART + 2 * CHUNK, WIDTH, cols), jnp.bfloat16),
            pltpu.SemaphoreType.DMA((sectors,)),
            pltpu.SemaphoreType.DMA((most,)),
        ],
        compiler_params=PARAMS,
        cost_estimate=pl.CostEstimate(
            flops=2 * PART * WIDTH * depth * cols, bytes_accessed=10 * 2**20, transcendentals=0
        ),
        name="right",
    )(jnp.stack([first_slot, z]).astype(jnp.int32), sizes, edge, site)


def product_kernel(scale, at_ref, size_ref, own_ref, other_ref, *rest):
    rights, rest = rest[:Z], rest[Z:]
    if scale is None:
        out_ref, one_buf, two_buf, sems = rest
    else:
        before_ref, out_ref, one_buf, two_buf, sems, before_buf = rest
    lo, core, z, row_first, col_first = (at_ref[k] for k in range(5))
    plan, _ = packed(size_ref, lo, lo + PART)
    copies = [
        pltpu.make_async_copy(own_ref, one_buf.at[pl.ds(core * HALF, HALF)], sems.at[0]),
        pltpu.make_async_copy(other_ref, one_buf.at[pl.ds((1 - core) * HALF, HALF)], sems.at[1]),
    ]
    for step in range(Z):
        base = lax.rem(z + Z - step, Z) * TWO
        copies.append(pltpu.make_async_copy(rights[step], two_buf.at[pl.ds(base, TWO)], sems.at[2 + step]))
    if scale is not None:
        copies.append(pltpu.make_async_copy(before_ref, before_buf, sems.at[2 + Z]))
    for copy in copies:
        copy.start()
    for k in range(CHUNK):
        one_buf[PART + k] = jnp.zeros(one_buf.shape[1:], one_buf.dtype)
    for copy in copies:
        copy.wait()
    rows, cols = out_ref.shape[1:]
    deep = lax.broadcasted_iota(jnp.int32, (CHUNK * WIDTH, cols), 0)
    row = lax.broadcasted_iota(jnp.int32, (rows, cols), 0) + row_first
    col = lax.broadcasted_iota(jnp.int32, (rows, cols), 1) + col_first
    for s in range(len(plan)):
        first, begin, end, _, chunks = plan[s]
        size = size_ref[s]
        deep_end = jnp.minimum(size, end * WIDTH)

        def add(c, total):
            block = begin + c * CHUNK
            q = first + block - lo
            left = jnp.concatenate([one_buf[q + k] for k in range(CHUNK)], axis=1)
            right = two_buf[pl.ds(q, CHUNK)].reshape(CHUNK * WIDTH, cols)
            right = jnp.where(deep < deep_end - block * WIDTH, right, jnp.bfloat16(0.0))
            return total + jnp.dot(left, right, preferred_element_type=jnp.float32)

        start = jnp.zeros((rows, cols), jnp.float32) if scale is None else before_buf[s]
        total = lax.fori_loop(0, chunks, add, start)
        if scale is None:
            out_ref[s] = total
        else:
            live = (row < size) & (col < size)
            out_ref[s] = jnp.where(live, total * jnp.float32(scale), jnp.float32(0.0)).astype(out_ref.dtype)


def product(scale, at, sizes, own, other, rights, *before):
    rows, cols, sectors = own.shape[1], rights[0].shape[2], sizes.shape[0]
    shape = (sectors, rows, cols)
    end = bool(before)
    return pl.pallas_call(
        lambda *refs: product_kernel(scale, *refs),
        out_shape=jax.ShapeDtypeStruct(shape, jnp.bfloat16 if end else jnp.float32),
        in_specs=[SMEM, SMEM] + [HBM] * (2 + Z + end),
        out_specs=VMEM,
        scratch_shapes=[
            pltpu.VMEM((PART + CHUNK, rows, WIDTH), jnp.bfloat16),
            pltpu.VMEM((PART + CHUNK, WIDTH, cols), jnp.bfloat16),
            pltpu.SemaphoreType.DMA((2 + Z + end,)),
        ]
        + [pltpu.VMEM(shape, jnp.float32)] * end,
        compiler_params=PARAMS,
        cost_estimate=pl.CostEstimate(
            flops=2 * PART * rows * WIDTH * cols, bytes_accessed=6 * 2**20, transcendentals=0
        ),
        name="product_end" if end else "product",
    )(at, sizes, own, other, *rights, *before)


def shift(array, axis, size, step):
    return lax.ppermute(array, axis, [(i, (i + step) % size) for i in range(size)])


def total(*terms):
    return sum(term.astype(jnp.float32) for term in terms).astype(jnp.bfloat16)


def over_z(arrays):
    return [shift(arrays[step], "z", Z, step) for step in range(1, Z)]


def over_y(array):
    return lax.all_to_all(array, "y", 0, 0, tiled=True)


def swap(array, axis):
    return shift(array, axis, 2, 1)


def on_device(edge_left, site_left, edge_right, site_right, sizes):
    order = site_left.shape[2]
    rows, cols = edge_left.shape[1], site_right.shape[2]
    z, xl, y, xh, core = (lax.axis_index(a) for a in ("z", "xl", "y", "xh", "core"))
    row_first = (z * XL + xl) * rows
    col_first = ((y * XH + xh) * CORE + core) * cols
    fence = lax.optimization_barrier
    A, B = 0, PART

    def left_sums(spread):
        return total(*spread.reshape((Y, ONE, rows, WIDTH)))

    def left_copies(own):
        return jnp.broadcast_to(own[None], (Y,) + own.shape).reshape(HALF, rows, WIDTH)

    def left_for_other(part, edges):
        return left_terms(part + (1 - core) * HALF, sizes, *edges)

    def left_chip(part, edges, came):
        return left_terms(part + core * HALF, sizes, *edges, came)

    left, right = (edge_left, site_left), (edge_right, site_right)
    goes = left_for_other(A, left)
    came = swap(goes, "core")
    goes, right = fence((goes, right))
    right_a = right_terms(jnp.int32(A), z, sizes, *right)
    right_a, left, came = fence((right_a, left, came))
    left_a = left_chip(A, left, came)

    right_a, left_a, left, right = fence((right_a, left_a, left, right))
    spread_a = over_y(left_a)
    came_a = over_z(right_a)
    goes = left_for_other(B, left)
    came = swap(goes, "core")
    goes, right = fence((goes, right))
    right_b = right_terms(jnp.int32(B), z, sizes, *right)
    right_b, left, came = fence((right_b, left, came))
    left_b = left_chip(B, left, came)
    spread_a, came_a, right_b, left_b = fence((spread_a, came_a, right_b, left_b))

    one_a, two_a = left_sums(spread_a), total(right_a[0], *came_a)
    one_a, two_a, right_b, left_b = fence((one_a, two_a, right_b, left_b))
    spread_b = over_y(left_b)
    came_b = over_z(right_b)
    one_x, two_x = swap(one_a, "xh"), swap(two_a, "xl")
    one_a, two_a = total(one_a, one_x), total(two_a, two_x)
    copies_a = left_copies(one_a)
    spread_b, came_b, copies_a, two_a = fence((spread_b, came_b, copies_a, two_a))

    one_b, two_b = left_sums(spread_b), total(right_b[0], *came_b)
    one_b, two_b, copies_a, two_a = fence((one_b, two_b, copies_a, two_a))
    half_a = over_y(copies_a)
    rights_a = [two_a] + over_z([two_a] * Z)
    one_x, two_x = swap(one_b, "xh"), swap(two_b, "xl")
    one_b, two_b = total(one_b, one_x), total(two_b, two_x)
    copies_b = left_copies(one_b)
    half_a, rights_a, copies_b, two_b = fence((half_a, rights_a, copies_b, two_b))

    at = jnp.stack([jnp.int32(A), core, z, row_first, col_first]).astype(jnp.int32)
    half_b = over_y(copies_b)
    rights_b = [two_b] + over_z([two_b] * Z)
    product_a = product(None, at, sizes, half_a, swap(half_a, "core"), rights_a)
    half_b, rights_b, product_a = fence((half_b, rights_b, product_a))
    at = at + jnp.array([B - A, 0, 0, 0, 0], jnp.int32)
    return product(order ** (-0.5), at, sizes, half_b, swap(half_b, "core"), rights_b, product_a)


def solution(mesh):
    split = Mesh(mesh.devices.reshape(Z, XL, Y, XH, CORE), ("z", "xl", "y", "xh", "core"))
    row, col = ("z", "xl"), ("y", "xh", "core")
    placed = (P(None, row, col), P(None, col, None), P(None, None, row), P(None, row, col), P())
    return jax.shard_map(
        on_device, mesh=split, in_specs=placed, out_specs=P(None, row, col), check_vma=False
    )
```

```python
import jax
import jax.numpy as jnp
from jax import lax
from jax.experimental import pallas as pl
from jax.experimental.pallas import tpu as pltpu
from jax.sharding import Mesh
from jax.sharding import PartitionSpec as P

WIDTH = 128
PART = 40
CHUNK = 4
Z, XL, Y, XH, CORE = 4, 2, 4, 2, 2
HALF = PART // CORE
ONE = HALF // Y
TWO = PART // Z
HBM = pl.BlockSpec(memory_space=pltpu.HBM)
ANY = pl.BlockSpec(memory_space=pl.ANY)
VMEM = pl.BlockSpec(memory_space=pltpu.VMEM)
SMEM = pl.BlockSpec(memory_space=pltpu.SMEM)
PARAMS = pltpu.CompilerParams(vmem_limit_bytes=60 * 2**20)


def packed(size_ref, lo, hi):
    first, chunk, plan = 0, 0, []
    for s in range(size_ref.shape[0]):
        blocks = lax.shift_right_logical(size_ref[s] + (WIDTH - 1), 7)
        begin, end = jnp.clip(lo - first, 0, blocks), jnp.clip(hi - first, 0, blocks)
        chunks = lax.shift_right_logical(end - begin + (CHUNK - 1), 2)
        plan.append((first, begin, end, chunk, chunks))
        first, chunk = first + blocks, chunk + chunks
    return plan, first


def most_chunks(slots, sectors):
    return (slots + sectors * (CHUNK - 1)) // CHUNK


def left_kernel(at_ref, size_ref, edge_ref, site_ref, *rest):
    outs, (out_buf, edge_buf, site_buf, edge_sem, site_sem, out_sem) = rest[: 2 * CORE], rest[2 * CORE :]
    core = at_ref[0]
    plan, used = packed(size_ref, 0, 2 * PART)
    def fetch(s, c):
        at = plan[s][3] + c
        columns = pl.ds(pl.multiple_of(c * (CHUNK * WIDTH), CHUNK * WIDTH), CHUNK * WIDTH)
        return pltpu.make_async_copy(site_ref.at[s, :, columns], site_buf.at[at], site_sem.at[at])

    edges = [pltpu.make_async_copy(edge_ref.at[s], edge_buf.at[s], edge_sem.at[s]) for s in range(len(plan))]
    for s in range(len(plan)):
        edges[s].start()

        @pl.loop(0, plan[s][4])
        def _(c):
            fetch(s, c).start()

    for s in range(len(plan)):
        first, _, _, chunk, chunks = plan[s]
        edges[s].wait()

        @pl.loop(0, chunks)
        def _(c):
            fetch(s, c).wait()
            term = jnp.dot(edge_buf[s], site_buf[chunk + c], preferred_element_type=jnp.float32)
            for k in range(CHUNK):
                out_buf[first + c * CHUNK + k] = term[:, k * WIDTH : (k + 1) * WIDTH].astype(out_buf.dtype)

    @pl.loop(used, 2 * PART)
    def _(q):
        out_buf[q] = jnp.zeros(out_buf.shape[1:], out_buf.dtype)

    copies = [
        pltpu.make_async_copy(
            out_buf.at[pl.ds(part * PART + which * HALF, HALF)], outs[part * CORE + k], out_sem.at[part * CORE + k]
        )
        for part in range(2)
        for k, which in enumerate((1 - core, core))
    ]
    for copy in copies:
        copy.start()
    for copy in copies:
        copy.wait()


def left_terms(core, sizes, edge, site):
    sectors, rows, depth = edge.shape
    most = most_chunks(2 * PART - 2, sectors)
    return pl.pallas_call(
        left_kernel,
        out_shape=[jax.ShapeDtypeStruct((HALF, rows, WIDTH), jnp.bfloat16)] * (2 * CORE),
        in_specs=[SMEM, SMEM, HBM, HBM],
        out_specs=[ANY] * (2 * CORE),
        scratch_shapes=[
            pltpu.VMEM((2 * PART + CHUNK, rows, WIDTH), jnp.bfloat16),
            pltpu.VMEM((sectors, rows, depth), jnp.bfloat16),
            pltpu.VMEM((most, depth, CHUNK * WIDTH), jnp.bfloat16),
            pltpu.SemaphoreType.DMA((sectors,)),
            pltpu.SemaphoreType.DMA((most,)),
            pltpu.SemaphoreType.DMA((2 * CORE,)),
        ],
        compiler_params=PARAMS,
        cost_estimate=pl.CostEstimate(
            flops=4 * PART * rows * depth * WIDTH, bytes_accessed=12 * 2**20, transcendentals=0
        ),
        name="left",
    )(core.reshape(1).astype(jnp.int32), sizes, edge, site)


def right_kernel(lo, at_ref, size_ref, edge_ref, site_ref, *rest):
    outs, (site_buf, edge_buf, term_buf, site_sem, edge_sem) = rest[:Z], rest[Z:]
    z = at_ref[0]
    plan, _ = packed(size_ref, lo, lo + PART)
    last = edge_ref.shape[1] // WIDTH - CHUNK

    def block_of(s, c):
        return jnp.minimum(plan[s][1] + c * CHUNK, last)

    def fetch(s, c):
        at = plan[s][3] + c
        rows = pl.ds(pl.multiple_of(block_of(s, c) * WIDTH, WIDTH), CHUNK * WIDTH)
        return pltpu.make_async_copy(edge_ref.at[s, rows, :], edge_buf.at[at], edge_sem.at[at])

    sites = [pltpu.make_async_copy(site_ref.at[s], site_buf.at[s], site_sem.at[s]) for s in range(len(plan))]
    for s in range(len(plan)):
        pl.when(plan[s][4] > 0)(sites[s].start)

        @pl.loop(0, plan[s][4])
        def _(c):
            fetch(s, c).start()

    for s in range(len(plan)):
        first, _, _, chunk, chunks = plan[s]
        pl.when(chunks > 0)(sites[s].wait)

        @pl.loop(0, chunks)
        def _(c):
            fetch(s, c).wait()
            term = jnp.dot(edge_buf[chunk + c], site_buf[s], preferred_element_type=jnp.float32)
            q = first + block_of(s, c) - lo + CHUNK
            term_buf[pl.ds(q, CHUNK)] = term.astype(jnp.bfloat16).reshape(CHUNK, WIDTH, term.shape[1])

    for step in range(Z):
        base = lax.rem(z + step, Z) * TWO + CHUNK
        for k in range(0, TWO, 2):
            outs[step][k : k + 2] = term_buf[pl.ds(base + k, 2)]


def right_terms(part, z, sizes, edge, site):
    sectors, depth, cols = site.shape
    most = most_chunks(PART, sectors)
    return pl.pallas_call(
        lambda *refs: right_kernel(part, *refs),
        out_shape=[jax.ShapeDtypeStruct((TWO, WIDTH, cols), jnp.bfloat16)] * Z,
        in_specs=[SMEM, SMEM, HBM, HBM],
        out_specs=[VMEM] * Z,
        scratch_shapes=[
            pltpu.VMEM((sectors, depth, cols), jnp.bfloat16),
            pltpu.VMEM((most, CHUNK * WIDTH, depth), jnp.bfloat16),
            pltpu.VMEM((PART + 2 * CHUNK, WIDTH, cols), jnp.bfloat16),
            pltpu.SemaphoreType.DMA((sectors,)),
            pltpu.SemaphoreType.DMA((most,)),
        ],
        compiler_params=PARAMS,
        cost_estimate=pl.CostEstimate(
            flops=2 * PART * WIDTH * depth * cols, bytes_accessed=10 * 2**20, transcendentals=0
        ),
        name="right",
    )(z.reshape(1).astype(jnp.int32), sizes, edge, site)


def product_kernel(lo, scale, at_ref, size_ref, own_ref, other_ref, *rest):
    rights, rest = rest[:Z], rest[Z:]
    if scale is None:
        out_ref, one_buf, two_buf, sems = rest
    else:
        before_ref, out_ref, one_buf, two_buf, sems, before_buf = rest
    core, z, row_first, col_first = (at_ref[k] for k in range(4))
    plan, _ = packed(size_ref, lo, lo + PART)
    copies = [
        pltpu.make_async_copy(own_ref, one_buf.at[pl.ds(core * HALF, HALF)], sems.at[0]),
        pltpu.make_async_copy(other_ref, one_buf.at[pl.ds((1 - core) * HALF, HALF)], sems.at[1]),
    ]
    for step in range(Z):
        base = lax.rem(z + Z - step, Z) * TWO
        copies.append(pltpu.make_async_copy(rights[step], two_buf.at[pl.ds(base, TWO)], sems.at[2 + step]))
    if scale is not None:
        copies.append(pltpu.make_async_copy(before_ref, before_buf, sems.at[2 + Z]))
    for copy in copies:
        copy.start()
    for k in range(CHUNK):
        one_buf[PART + k] = jnp.zeros(one_buf.shape[1:], one_buf.dtype)
    for copy in copies:
        copy.wait()
    rows, cols = out_ref.shape[1:]
    deep = lax.broadcasted_iota(jnp.int32, (CHUNK * WIDTH, cols), 0)
    row = lax.broadcasted_iota(jnp.int32, (rows, cols), 0) + row_first
    col = lax.broadcasted_iota(jnp.int32, (rows, cols), 1) + col_first
    for s in range(len(plan)):
        first, begin, end, _, chunks = plan[s]
        size = size_ref[s]
        deep_end = jnp.minimum(size, end * WIDTH)

        def add(c, total):
            block = begin + c * CHUNK
            q = first + block - lo
            left = jnp.concatenate([one_buf[q + k] for k in range(CHUNK)], axis=1)
            right = two_buf[pl.ds(q, CHUNK)].reshape(CHUNK * WIDTH, cols)
            right = jnp.where(deep < deep_end - block * WIDTH, right, jnp.bfloat16(0.0))
            return total + jnp.dot(left, right, preferred_element_type=jnp.float32)

        start = jnp.zeros((rows, cols), jnp.float32) if scale is None else before_buf[s]
        total = lax.fori_loop(0, chunks, add, start)
        if scale is None:
            out_ref[s] = total
        else:
            live = (row < size) & (col < size)
            out_ref[s] = jnp.where(live, total * jnp.float32(scale), jnp.float32(0.0)).astype(out_ref.dtype)


def product(part, scale, at, sizes, own, other, rights, *before):
    rows, cols, sectors = own.shape[1], rights[0].shape[2], sizes.shape[0]
    shape = (sectors, rows, cols)
    end = bool(before)
    return pl.pallas_call(
        lambda *refs: product_kernel(part, scale, *refs),
        out_shape=jax.ShapeDtypeStruct(shape, jnp.bfloat16 if end else jnp.float32),
        in_specs=[SMEM, SMEM] + [ANY] * (2 + Z + end),
        out_specs=VMEM,
        scratch_shapes=[
            pltpu.VMEM((PART + CHUNK, rows, WIDTH), jnp.bfloat16),
            pltpu.VMEM((PART + CHUNK, WIDTH, cols), jnp.bfloat16),
            pltpu.SemaphoreType.DMA((2 + Z + end,)),
        ]
        + [pltpu.VMEM(shape, jnp.float32)] * end,
        compiler_params=PARAMS,
        cost_estimate=pl.CostEstimate(
            flops=2 * PART * rows * WIDTH * cols, bytes_accessed=6 * 2**20, transcendentals=0
        ),
        name="product_end" if end else "product",
    )(at, sizes, own, other, *rights, *before)


def shift(array, axis, size, step):
    return lax.ppermute(array, axis, [(i, (i + step) % size) for i in range(size)])


def total(*terms):
    return sum(term.astype(jnp.float32) for term in terms).astype(jnp.bfloat16)


def over_z(arrays):
    return [shift(arrays[step], "z", Z, step) for step in range(1, Z)]


def over_y(array):
    return lax.all_to_all(array, "y", 0, 0, tiled=True)


def swap(array, axis):
    return shift(array, axis, 2, 1)


def on_device(edge_left, site_left, edge_right, site_right, sizes):
    order = site_left.shape[2]
    rows, cols = edge_left.shape[1], site_right.shape[2]
    z, xl, y, xh, core = (lax.axis_index(a) for a in ("z", "xl", "y", "xh", "core"))
    row_first = (z * XL + xl) * rows
    col_first = ((y * XH + xh) * CORE + core) * cols
    fence = lax.optimization_barrier
    A, B = 0, PART

    def left_sums(spread):
        return total(*spread.reshape((Y, ONE, rows, WIDTH)))

    def left_copies(own):
        return jnp.broadcast_to(own[None], (Y,) + own.shape).reshape(HALF, rows, WIDTH)

    goes_a, keeps_a, goes_b, keeps_b = left_terms(core, sizes, edge_left, site_left)
    came_a, came_b = swap(goes_a, "core"), swap(goes_b, "core")
    goes_a, right = fence((goes_a, (edge_right, site_right)))
    right_a = right_terms(A, z, sizes, *right)
    right_a, right, came_a = fence((right_a, right, came_a))
    left_a = total(keeps_a, came_a)

    came_a = over_z(right_a)
    left_a, right, keeps_b = fence((left_a, right, keeps_b))
    spread_a = over_y(left_a)
    right_b = right_terms(B, z, sizes, *right)
    left_b = total(keeps_b, came_b)
    spread_a, came_a, right_b, left_b = fence((spread_a, came_a, right_b, left_b))

    came_b = over_z(right_b)
    one_a, two_a = left_sums(spread_a), total(right_a[0], *came_a)
    one_a, two_a, left_b = fence((one_a, two_a, left_b))
    spread_b = over_y(left_b)
    one_x, two_x = swap(one_a, "xh"), swap(two_a, "xl")
    one_a, two_a = total(one_a, one_x), total(two_a, two_x)
    spread_b, came_b, one_a, two_a = fence((spread_b, came_b, one_a, two_a))

    rights_a = [two_a] + over_z([two_a] * Z)
    copies_a = left_copies(one_a)
    one_b, two_b = left_sums(spread_b), total(right_b[0], *came_b)
    one_b, two_b, copies_a = fence((one_b, two_b, copies_a))
    half_a = over_y(copies_a)
    one_x, two_x = swap(one_b, "xh"), swap(two_b, "xl")
    one_b, two_b = total(one_b, one_x), total(two_b, two_x)
    half_a, rights_a, one_b, two_b = fence((half_a, rights_a, one_b, two_b))

    rights_b = [two_b] + over_z([two_b] * Z)
    at = jnp.stack([core, z, row_first, col_first]).astype(jnp.int32)
    half_b = over_y(left_copies(one_b))
    product_a = product(A, None, at, sizes, half_a, swap(half_a, "core"), rights_a)
    half_b, rights_b, product_a = fence((half_b, rights_b, product_a))
    return product(B, order ** (-0.5), at, sizes, half_b, swap(half_b, "core"), rights_b, product_a)


def solution(mesh):
    split = Mesh(mesh.devices.reshape(Z, XL, Y, XH, CORE), ("z", "xl", "y", "xh", "core"))
    row, col = ("z", "xl"), ("y", "xh", "core")
    placed = (P(None, row, col), P(None, col, None), P(None, None, row), P(None, row, col), P())
    return jax.shard_map(
        on_device, mesh=split, in_specs=placed, out_specs=P(None, row, col), check_vma=False
    )
```

```python
import jax
import jax.numpy as jnp
from jax import lax
from jax.experimental import pallas as pl
from jax.experimental.pallas import tpu as pltpu
from jax.sharding import Mesh
from jax.sharding import PartitionSpec as P

WIDTH = 128
PART = 40
CHUNK = 4
Z, XL, Y, XH, CORE = 4, 2, 4, 2, 2
HALF = PART // CORE
ONE = HALF // Y
TWO = PART // Z
HBM = pl.BlockSpec(memory_space=pltpu.HBM)
ANY = pl.BlockSpec(memory_space=pl.ANY)
VMEM = pl.BlockSpec(memory_space=pltpu.VMEM)
SMEM = pl.BlockSpec(memory_space=pltpu.SMEM)
PARAMS = pltpu.CompilerParams(vmem_limit_bytes=60 * 2**20)


def packed(size_ref, lo, hi):
    first, chunk, plan = 0, 0, []
    for s in range(size_ref.shape[0]):
        blocks = lax.shift_right_logical(size_ref[s] + (WIDTH - 1), 7)
        begin, end = jnp.clip(lo - first, 0, blocks), jnp.clip(hi - first, 0, blocks)
        chunks = lax.shift_right_logical(end - begin + (CHUNK - 1), 2)
        plan.append((first, begin, end, chunk, chunks))
        first, chunk = first + blocks, chunk + chunks
    return plan, first


def most_chunks(slots, sectors):
    return (slots + sectors * (CHUNK - 1)) // CHUNK


def left_kernel(at_ref, size_ref, edge_ref, site_ref, *rest):
    outs, (out_buf, edge_buf, site_buf, edge_sem, site_sem, out_sem) = rest[: 2 * CORE], rest[2 * CORE :]
    core = at_ref[0]
    plan, used = packed(size_ref, 0, 2 * PART)
    def fetch(s, c):
        at = plan[s][3] + c
        columns = pl.ds(pl.multiple_of(c * (CHUNK * WIDTH), CHUNK * WIDTH), CHUNK * WIDTH)
        return pltpu.make_async_copy(site_ref.at[s, :, columns], site_buf.at[at], site_sem.at[at])

    edges = [pltpu.make_async_copy(edge_ref.at[s], edge_buf.at[s], edge_sem.at[s]) for s in range(len(plan))]
    for s in range(len(plan)):
        edges[s].start()

        @pl.loop(0, plan[s][4])
        def _(c):
            fetch(s, c).start()

    for s in range(len(plan)):
        first, _, _, chunk, chunks = plan[s]
        edges[s].wait()

        @pl.loop(0, chunks)
        def _(c):
            fetch(s, c).wait()
            term = jnp.dot(edge_buf[s], site_buf[chunk + c], preferred_element_type=jnp.float32)
            for k in range(CHUNK):
                out_buf[first + c * CHUNK + k] = term[:, k * WIDTH : (k + 1) * WIDTH].astype(out_buf.dtype)

    @pl.loop(used, 2 * PART)
    def _(q):
        out_buf[q] = jnp.zeros(out_buf.shape[1:], out_buf.dtype)

    copies = [
        pltpu.make_async_copy(
            out_buf.at[pl.ds(part * PART + which * HALF, HALF)], outs[part * CORE + k], out_sem.at[part * CORE + k]
        )
        for part in range(2)
        for k, which in enumerate((1 - core, core))
    ]
    for copy in copies:
        copy.start()
    for copy in copies:
        copy.wait()


def left_terms(core, sizes, edge, site):
    sectors, rows, depth = edge.shape
    most = most_chunks(2 * PART - 2, sectors)
    return pl.pallas_call(
        left_kernel,
        out_shape=[jax.ShapeDtypeStruct((HALF, rows, WIDTH), jnp.bfloat16)] * (2 * CORE),
        in_specs=[SMEM, SMEM, HBM, HBM],
        out_specs=[ANY] * (2 * CORE),
        scratch_shapes=[
            pltpu.VMEM((2 * PART + CHUNK, rows, WIDTH), jnp.bfloat16),
            pltpu.VMEM((sectors, rows, depth), jnp.bfloat16),
            pltpu.VMEM((most, depth, CHUNK * WIDTH), jnp.bfloat16),
            pltpu.SemaphoreType.DMA((sectors,)),
            pltpu.SemaphoreType.DMA((most,)),
            pltpu.SemaphoreType.DMA((2 * CORE,)),
        ],
        compiler_params=PARAMS,
        cost_estimate=pl.CostEstimate(
            flops=4 * PART * rows * depth * WIDTH, bytes_accessed=12 * 2**20, transcendentals=0
        ),
        name="left",
    )(core.reshape(1).astype(jnp.int32), sizes, edge, site)


def right_kernel(lo, at_ref, size_ref, edge_ref, site_ref, *rest):
    outs, (site_buf, edge_buf, term_buf, site_sem, edge_sem) = rest[:Z], rest[Z:]
    z = at_ref[0]
    plan, _ = packed(size_ref, lo, lo + PART)
    last = edge_ref.shape[1] // WIDTH - CHUNK

    def block_of(s, c):
        return jnp.minimum(plan[s][1] + c * CHUNK, last)

    def fetch(s, c):
        at = plan[s][3] + c
        rows = pl.ds(pl.multiple_of(block_of(s, c) * WIDTH, WIDTH), CHUNK * WIDTH)
        return pltpu.make_async_copy(edge_ref.at[s, rows, :], edge_buf.at[at], edge_sem.at[at])

    sites = [pltpu.make_async_copy(site_ref.at[s], site_buf.at[s], site_sem.at[s]) for s in range(len(plan))]
    for s in range(len(plan)):
        pl.when(plan[s][4] > 0)(sites[s].start)

        @pl.loop(0, plan[s][4])
        def _(c):
            fetch(s, c).start()

    for s in range(len(plan)):
        first, _, _, chunk, chunks = plan[s]
        pl.when(chunks > 0)(sites[s].wait)

        @pl.loop(0, chunks)
        def _(c):
            fetch(s, c).wait()
            term = jnp.dot(edge_buf[chunk + c], site_buf[s], preferred_element_type=jnp.float32)
            q = first + block_of(s, c) - lo + CHUNK
            term_buf[pl.ds(q, CHUNK)] = term.astype(jnp.bfloat16).reshape(CHUNK, WIDTH, term.shape[1])

    for step in range(Z):
        base = lax.rem(z + step, Z) * TWO + CHUNK
        for k in range(0, TWO, 2):
            outs[step][k : k + 2] = term_buf[pl.ds(base + k, 2)]


def right_terms(part, z, sizes, edge, site):
    sectors, depth, cols = site.shape
    most = most_chunks(PART, sectors)
    return pl.pallas_call(
        lambda *refs: right_kernel(part, *refs),
        out_shape=[jax.ShapeDtypeStruct((TWO, WIDTH, cols), jnp.bfloat16)] * Z,
        in_specs=[SMEM, SMEM, HBM, HBM],
        out_specs=[VMEM] * Z,
        scratch_shapes=[
            pltpu.VMEM((sectors, depth, cols), jnp.bfloat16),
            pltpu.VMEM((most, CHUNK * WIDTH, depth), jnp.bfloat16),
            pltpu.VMEM((PART + 2 * CHUNK, WIDTH, cols), jnp.bfloat16),
            pltpu.SemaphoreType.DMA((sectors,)),
            pltpu.SemaphoreType.DMA((most,)),
        ],
        compiler_params=PARAMS,
        cost_estimate=pl.CostEstimate(
            flops=2 * PART * WIDTH * depth * cols, bytes_accessed=10 * 2**20, transcendentals=0
        ),
        name="right",
    )(z.reshape(1).astype(jnp.int32), sizes, edge, site)


def product_kernel(lo, scale, at_ref, size_ref, own_ref, other_ref, *rest):
    rights, rest = rest[:Z], rest[Z:]
    if scale is None:
        out_ref, one_buf, two_buf, sems = rest
    else:
        before_ref, out_ref, one_buf, two_buf, sems, before_buf = rest
    core, z, row_first, col_first = (at_ref[k] for k in range(4))
    plan, _ = packed(size_ref, lo, lo + PART)
    copies = [
        pltpu.make_async_copy(own_ref, one_buf.at[pl.ds(core * HALF, HALF)], sems.at[0]),
        pltpu.make_async_copy(other_ref, one_buf.at[pl.ds((1 - core) * HALF, HALF)], sems.at[1]),
    ]
    for step in range(Z):
        base = lax.rem(z + Z - step, Z) * TWO
        copies.append(pltpu.make_async_copy(rights[step], two_buf.at[pl.ds(base, TWO)], sems.at[2 + step]))
    if scale is not None:
        copies.append(pltpu.make_async_copy(before_ref, before_buf, sems.at[2 + Z]))
    for copy in copies:
        copy.start()
    for k in range(CHUNK):
        one_buf[PART + k] = jnp.zeros(one_buf.shape[1:], one_buf.dtype)
    for copy in copies:
        copy.wait()
    rows, cols = out_ref.shape[1:]
    deep = lax.broadcasted_iota(jnp.int32, (CHUNK * WIDTH, cols), 0)
    row = lax.broadcasted_iota(jnp.int32, (rows, cols), 0) + row_first
    col = lax.broadcasted_iota(jnp.int32, (rows, cols), 1) + col_first
    for s in range(len(plan)):
        first, begin, end, _, chunks = plan[s]
        size = size_ref[s]
        deep_end = jnp.minimum(size, end * WIDTH)

        def add(c, total):
            block = begin + c * CHUNK
            q = first + block - lo
            left = jnp.concatenate([one_buf[q + k] for k in range(CHUNK)], axis=1)
            right = two_buf[pl.ds(q, CHUNK)].reshape(CHUNK * WIDTH, cols)
            right = jnp.where(deep < deep_end - block * WIDTH, right, jnp.bfloat16(0.0))
            return total + jnp.dot(left, right, preferred_element_type=jnp.float32)

        start = jnp.zeros((rows, cols), jnp.float32) if scale is None else before_buf[s]
        total = lax.fori_loop(0, chunks, add, start)
        if scale is None:
            out_ref[s] = total
        else:
            live = (row < size) & (col < size)
            out_ref[s] = jnp.where(live, total * jnp.float32(scale), jnp.float32(0.0)).astype(out_ref.dtype)


def product(part, scale, at, sizes, own, other, rights, *before):
    rows, cols, sectors = own.shape[1], rights[0].shape[2], sizes.shape[0]
    shape = (sectors, rows, cols)
    end = bool(before)
    return pl.pallas_call(
        lambda *refs: product_kernel(part, scale, *refs),
        out_shape=jax.ShapeDtypeStruct(shape, jnp.bfloat16 if end else jnp.float32),
        in_specs=[SMEM, SMEM] + [ANY] * (2 + Z + end),
        out_specs=VMEM,
        scratch_shapes=[
            pltpu.VMEM((PART + CHUNK, rows, WIDTH), jnp.bfloat16),
            pltpu.VMEM((PART + CHUNK, WIDTH, cols), jnp.bfloat16),
            pltpu.SemaphoreType.DMA((2 + Z + end,)),
        ]
        + [pltpu.VMEM(shape, jnp.float32)] * end,
        compiler_params=pltpu.CompilerParams(vmem_limit_bytes=16 * 2**20),
        cost_estimate=pl.CostEstimate(
            flops=2 * PART * rows * WIDTH * cols, bytes_accessed=6 * 2**20, transcendentals=0
        ),
        name="product_end" if end else "product",
    )(at, sizes, own, other, *rights, *before)


def shift(array, axis, size, step):
    return lax.ppermute(array, axis, [(i, (i + step) % size) for i in range(size)])


def total(*terms):
    return sum(term.astype(jnp.float32) for term in terms).astype(jnp.bfloat16)


def over_z(arrays):
    return [shift(arrays[step], "z", Z, step) for step in range(1, Z)]


def over_y(array):
    return lax.all_to_all(array, "y", 0, 0, tiled=True)


def swap(array, axis):
    return shift(array, axis, 2, 1)


def on_device(edge_left, site_left, edge_right, site_right, sizes):
    order = site_left.shape[2]
    rows, cols = edge_left.shape[1], site_right.shape[2]
    z, xl, y, xh, core = (lax.axis_index(a) for a in ("z", "xl", "y", "xh", "core"))
    row_first = (z * XL + xl) * rows
    col_first = ((y * XH + xh) * CORE + core) * cols
    fence = lax.optimization_barrier
    A, B = 0, PART

    def left_sums(spread):
        return total(*spread.reshape((Y, ONE, rows, WIDTH)))

    def left_copies(own):
        return jnp.broadcast_to(own[None], (Y,) + own.shape).reshape(HALF, rows, WIDTH)

    goes_a, keeps_a, goes_b, keeps_b = left_terms(core, sizes, edge_left, site_left)
    came_a, came_b = swap(goes_a, "core"), swap(goes_b, "core")
    goes_a, right = fence((goes_a, (edge_right, site_right)))
    right_a = right_terms(A, z, sizes, *right)
    right_a, right, came_a = fence((right_a, right, came_a))
    left_a = total(keeps_a, came_a)

    came_a = over_z(right_a)
    left_a, right, keeps_b = fence((left_a, right, keeps_b))
    spread_a = over_y(left_a)
    right_b = right_terms(B, z, sizes, *right)
    left_b = total(keeps_b, came_b)
    spread_a, right_b, left_b = fence((spread_a, right_b, left_b))

    came_b = over_z(right_b)
    one_a, two_a = left_sums(spread_a), total(right_a[0], *came_a)
    one_a, left_b = fence((one_a, left_b))
    spread_b = over_y(left_b)
    one_x, two_x = swap(one_a, "xh"), swap(two_a, "xl")
    one_a, two_a = total(one_a, one_x), total(two_a, two_x)
    spread_b, one_a, two_a = fence((spread_b, one_a, two_a))

    rights_a = [two_a] + over_z([two_a] * Z)
    copies_a = left_copies(one_a)
    one_b, two_b = left_sums(spread_b), total(right_b[0], *came_b)
    one_b, copies_a = fence((one_b, copies_a))
    half_a = over_y(copies_a)
    one_x, two_x = swap(one_b, "xh"), swap(two_b, "xl")
    one_b, two_b = total(one_b, one_x), total(two_b, two_x)
    half_a, rights_a, one_b, two_b = fence((half_a, rights_a, one_b, two_b))

    rights_b = [two_b] + over_z([two_b] * Z)
    at = jnp.stack([core, z, row_first, col_first]).astype(jnp.int32)
    half_b = over_y(left_copies(one_b))
    product_a = product(A, None, at, sizes, half_a, swap(half_a, "core"), rights_a)
    half_b, rights_b, product_a = fence((half_b, rights_b, product_a))
    return product(B, order ** (-0.5), at, sizes, half_b, swap(half_b, "core"), rights_b, product_a)


def solution(mesh):
    split = Mesh(mesh.devices.reshape(Z, XL, Y, XH, CORE), ("z", "xl", "y", "xh", "core"))
    row, col = ("z", "xl"), ("y", "xh", "core")
    placed = (P(None, row, col), P(None, col, None), P(None, None, row), P(None, row, col), P())
    return jax.shard_map(
        on_device, mesh=split, in_specs=placed, out_specs=P(None, row, col), check_vma=False
    )
```

```python
import jax
import jax.numpy as jnp
from jax import lax
from jax.experimental import pallas as pl
from jax.experimental.pallas import tpu as pltpu
from jax.sharding import Mesh
from jax.sharding import PartitionSpec as P

WIDTH = 128
PART = 40
CHUNK = 4
Z, XL, Y, XH, CORE = 4, 2, 4, 2, 2
HALF = PART // CORE
ONE = HALF // Y
TWO = PART // Z
HBM = pl.BlockSpec(memory_space=pltpu.HBM)
ANY = pl.BlockSpec(memory_space=pl.ANY)
VMEM = pl.BlockSpec(memory_space=pltpu.VMEM)
SMEM = pl.BlockSpec(memory_space=pltpu.SMEM)
PARAMS = pltpu.CompilerParams(vmem_limit_bytes=60 * 2**20)


def packed(size_ref, lo, hi):
    first, chunk, plan = 0, 0, []
    for s in range(size_ref.shape[0]):
        blocks = lax.shift_right_logical(size_ref[s] + (WIDTH - 1), 7)
        begin, end = jnp.clip(lo - first, 0, blocks), jnp.clip(hi - first, 0, blocks)
        chunks = lax.shift_right_logical(end - begin + (CHUNK - 1), 2)
        plan.append((first, begin, end, chunk, chunks))
        first, chunk = first + blocks, chunk + chunks
    return plan, first


def most_chunks(slots, sectors):
    return (slots + sectors * (CHUNK - 1)) // CHUNK


def left_kernel(at_ref, size_ref, edge_ref, site_ref, *rest):
    outs, (out_buf, edge_buf, site_buf, edge_sem, site_sem, out_sem) = rest[: 2 * CORE], rest[2 * CORE :]
    core = at_ref[0]
    plan, used = packed(size_ref, 0, 2 * PART)
    def fetch(s, c):
        at = plan[s][3] + c
        columns = pl.ds(pl.multiple_of(c * (CHUNK * WIDTH), CHUNK * WIDTH), CHUNK * WIDTH)
        return pltpu.make_async_copy(site_ref.at[s, :, columns], site_buf.at[at], site_sem.at[at])

    edges = [pltpu.make_async_copy(edge_ref.at[s], edge_buf.at[s], edge_sem.at[s]) for s in range(len(plan))]
    for s in range(len(plan)):
        edges[s].start()

        @pl.loop(0, plan[s][4])
        def _(c):
            fetch(s, c).start()

    def send(piece):
        part, which = divmod(piece, CORE)
        k = jnp.where(core == which, 1, 0)
        for to in range(CORE):
            copy = pltpu.make_async_copy(
                out_buf.at[pl.ds(piece * HALF, HALF)], outs[part * CORE + to], out_sem.at[part * CORE + to]
            )
            pl.when(k == to)(copy.start)

    for s in range(len(plan)):
        first, _, blocks, chunk, chunks = plan[s]
        edges[s].wait()

        @pl.loop(0, chunks)
        def _(c):
            fetch(s, c).wait()
            term = jnp.dot(edge_buf[s], site_buf[chunk + c], preferred_element_type=jnp.float32)
            for k in range(CHUNK):
                out_buf[first + c * CHUNK + k] = term[:, k * WIDTH : (k + 1) * WIDTH].astype(out_buf.dtype)

        for piece in range(2 * CORE):
            edge = (piece + 1) * HALF
            pl.when((first < edge) & (first + blocks >= edge))(lambda piece=piece: send(piece))

    @pl.loop(used, 2 * PART)
    def _(q):
        out_buf[q] = jnp.zeros(out_buf.shape[1:], out_buf.dtype)

    for piece in range(2 * CORE):
        pl.when(used < (piece + 1) * HALF)(lambda piece=piece: send(piece))
    for k in range(2 * CORE):
        pltpu.make_async_copy(out_buf.at[pl.ds(0, HALF)], outs[k], out_sem.at[k]).wait()


def left_terms(core, sizes, edge, site):
    sectors, rows, depth = edge.shape
    most = most_chunks(2 * PART - 2, sectors)
    return pl.pallas_call(
        left_kernel,
        out_shape=[jax.ShapeDtypeStruct((HALF, rows, WIDTH), jnp.bfloat16)] * (2 * CORE),
        in_specs=[SMEM, SMEM, HBM, HBM],
        out_specs=[ANY] * (2 * CORE),
        scratch_shapes=[
            pltpu.VMEM((2 * PART + CHUNK, rows, WIDTH), jnp.bfloat16),
            pltpu.VMEM((sectors, rows, depth), jnp.bfloat16),
            pltpu.VMEM((most, depth, CHUNK * WIDTH), jnp.bfloat16),
            pltpu.SemaphoreType.DMA((sectors,)),
            pltpu.SemaphoreType.DMA((most,)),
            pltpu.SemaphoreType.DMA((2 * CORE,)),
        ],
        compiler_params=PARAMS,
        cost_estimate=pl.CostEstimate(
            flops=4 * PART * rows * depth * WIDTH, bytes_accessed=12 * 2**20, transcendentals=0
        ),
        name="left",
    )(core.reshape(1).astype(jnp.int32), sizes, edge, site)


def right_kernel(lo, at_ref, size_ref, edge_ref, site_ref, *rest):
    outs, (site_buf, edge_buf, term_buf, site_sem, edge_sem) = rest[:Z], rest[Z:]
    z = at_ref[0]
    plan, _ = packed(size_ref, lo, lo + PART)
    last = edge_ref.shape[1] // WIDTH - CHUNK

    def block_of(s, c):
        return jnp.minimum(plan[s][1] + c * CHUNK, last)

    def fetch(s, c):
        at = plan[s][3] + c
        rows = pl.ds(pl.multiple_of(block_of(s, c) * WIDTH, WIDTH), CHUNK * WIDTH)
        return pltpu.make_async_copy(edge_ref.at[s, rows, :], edge_buf.at[at], edge_sem.at[at])

    sites = [pltpu.make_async_copy(site_ref.at[s], site_buf.at[s], site_sem.at[s]) for s in range(len(plan))]
    for s in range(len(plan)):
        pl.when(plan[s][4] > 0)(sites[s].start)

        @pl.loop(0, plan[s][4])
        def _(c):
            fetch(s, c).start()

    for s in range(len(plan)):
        first, _, _, chunk, chunks = plan[s]
        pl.when(chunks > 0)(sites[s].wait)

        @pl.loop(0, chunks)
        def _(c):
            fetch(s, c).wait()
            term = jnp.dot(edge_buf[chunk + c], site_buf[s], preferred_element_type=jnp.float32)
            q = first + block_of(s, c) - lo + CHUNK
            term_buf[pl.ds(q, CHUNK)] = term.astype(jnp.bfloat16).reshape(CHUNK, WIDTH, term.shape[1])

    for step in range(Z):
        base = lax.rem(z + step, Z) * TWO + CHUNK
        for k in range(0, TWO, 2):
            outs[step][k : k + 2] = term_buf[pl.ds(base + k, 2)]


def right_terms(part, z, sizes, edge, site):
    sectors, depth, cols = site.shape
    most = most_chunks(PART, sectors)
    return pl.pallas_call(
        lambda *refs: right_kernel(part, *refs),
        out_shape=[jax.ShapeDtypeStruct((TWO, WIDTH, cols), jnp.bfloat16)] * Z,
        in_specs=[SMEM, SMEM, HBM, HBM],
        out_specs=[VMEM] * Z,
        scratch_shapes=[
            pltpu.VMEM((sectors, depth, cols), jnp.bfloat16),
            pltpu.VMEM((most, CHUNK * WIDTH, depth), jnp.bfloat16),
            pltpu.VMEM((PART + 2 * CHUNK, WIDTH, cols), jnp.bfloat16),
            pltpu.SemaphoreType.DMA((sectors,)),
            pltpu.SemaphoreType.DMA((most,)),
        ],
        compiler_params=PARAMS,
        cost_estimate=pl.CostEstimate(
            flops=2 * PART * WIDTH * depth * cols, bytes_accessed=10 * 2**20, transcendentals=0
        ),
        name="right",
    )(z.reshape(1).astype(jnp.int32), sizes, edge, site)


def product_kernel(lo, scale, at_ref, size_ref, own_ref, other_ref, *rest):
    rights, rest = rest[:Z], rest[Z:]
    if scale is None:
        out_ref, one_buf, two_buf, sems = rest
    else:
        before_ref, out_ref, one_buf, two_buf, sems, before_buf = rest
    core, z, row_first, col_first = (at_ref[k] for k in range(4))
    plan, _ = packed(size_ref, lo, lo + PART)
    copies = [
        pltpu.make_async_copy(own_ref, one_buf.at[pl.ds(core * HALF, HALF)], sems.at[0]),
        pltpu.make_async_copy(other_ref, one_buf.at[pl.ds((1 - core) * HALF, HALF)], sems.at[1]),
    ]
    for step in range(Z):
        base = lax.rem(z + Z - step, Z) * TWO
        copies.append(pltpu.make_async_copy(rights[step], two_buf.at[pl.ds(base, TWO)], sems.at[2 + step]))
    if scale is not None:
        copies.append(pltpu.make_async_copy(before_ref, before_buf, sems.at[2 + Z]))
    for copy in copies:
        copy.start()
    for k in range(CHUNK):
        one_buf[PART + k] = jnp.zeros(one_buf.shape[1:], one_buf.dtype)
    for copy in copies:
        copy.wait()
    rows, cols = out_ref.shape[1:]
    deep = lax.broadcasted_iota(jnp.int32, (CHUNK * WIDTH, cols), 0)
    row = lax.broadcasted_iota(jnp.int32, (rows, cols), 0) + row_first
    col = lax.broadcasted_iota(jnp.int32, (rows, cols), 1) + col_first
    for s in range(len(plan)):
        first, begin, end, _, chunks = plan[s]
        size = size_ref[s]
        deep_end = jnp.minimum(size, end * WIDTH)

        def add(c, total):
            block = begin + c * CHUNK
            q = first + block - lo
            left = jnp.concatenate([one_buf[q + k] for k in range(CHUNK)], axis=1)
            right = two_buf[pl.ds(q, CHUNK)].reshape(CHUNK * WIDTH, cols)
            right = jnp.where(deep < deep_end - block * WIDTH, right, jnp.bfloat16(0.0))
            return total + jnp.dot(left, right, preferred_element_type=jnp.float32)

        start = jnp.zeros((rows, cols), jnp.float32) if scale is None else before_buf[s]
        total = lax.fori_loop(0, chunks, add, start)
        if scale is None:
            out_ref[s] = total
        else:
            live = (row < size) & (col < size)
            out_ref[s] = jnp.where(live, total * jnp.float32(scale), jnp.float32(0.0)).astype(out_ref.dtype)


def product(part, scale, at, sizes, own, other, rights, *before):
    rows, cols, sectors = own.shape[1], rights[0].shape[2], sizes.shape[0]
    shape = (sectors, rows, cols)
    end = bool(before)
    return pl.pallas_call(
        lambda *refs: product_kernel(part, scale, *refs),
        out_shape=jax.ShapeDtypeStruct(shape, jnp.bfloat16 if end else jnp.float32),
        in_specs=[SMEM, SMEM] + [ANY] * (2 + Z + end),
        out_specs=VMEM,
        scratch_shapes=[
            pltpu.VMEM((PART + CHUNK, rows, WIDTH), jnp.bfloat16),
            pltpu.VMEM((PART + CHUNK, WIDTH, cols), jnp.bfloat16),
            pltpu.SemaphoreType.DMA((2 + Z + end,)),
        ]
        + [pltpu.VMEM(shape, jnp.float32)] * end,
        compiler_params=pltpu.CompilerParams(vmem_limit_bytes=16 * 2**20),
        cost_estimate=pl.CostEstimate(
            flops=2 * PART * rows * WIDTH * cols, bytes_accessed=6 * 2**20, transcendentals=0
        ),
        name="product_end" if end else "product",
    )(at, sizes, own, other, *rights, *before)


def shift(array, axis, size, step):
    return lax.ppermute(array, axis, [(i, (i + step) % size) for i in range(size)])


def total(*terms):
    return sum(term.astype(jnp.float32) for term in terms).astype(jnp.bfloat16)


def over_z(arrays):
    return [shift(arrays[step], "z", Z, step) for step in range(1, Z)]


def over_y(array):
    return lax.all_to_all(array, "y", 0, 0, tiled=True)


def swap(array, axis):
    return shift(array, axis, 2, 1)


def on_device(edge_left, site_left, edge_right, site_right, sizes):
    order = site_left.shape[2]
    rows, cols = edge_left.shape[1], site_right.shape[2]
    z, xl, y, xh, core = (lax.axis_index(a) for a in ("z", "xl", "y", "xh", "core"))
    row_first = (z * XL + xl) * rows
    col_first = ((y * XH + xh) * CORE + core) * cols
    fence = lax.optimization_barrier
    A, B = 0, PART

    def left_sums(spread):
        return total(*spread.reshape((Y, ONE, rows, WIDTH)))

    def left_copies(own):
        return jnp.broadcast_to(own[None], (Y,) + own.shape).reshape(HALF, rows, WIDTH)

    goes_a, keeps_a, goes_b, keeps_b = left_terms(core, sizes, edge_left, site_left)
    came_a, came_b = swap(goes_a, "core"), swap(goes_b, "core")
    goes_a, right = fence((goes_a, (edge_right, site_right)))
    right_a = right_terms(A, z, sizes, *right)
    right_a, right, came_a = fence((right_a, right, came_a))
    left_a = total(keeps_a, came_a)

    came_a = over_z(right_a)
    left_a, right, keeps_b = fence((left_a, right, keeps_b))
    spread_a = over_y(left_a)
    right_b = right_terms(B, z, sizes, *right)
    left_b = total(keeps_b, came_b)
    spread_a, right_b, left_b = fence((spread_a, right_b, left_b))

    came_b = over_z(right_b)
    one_a, two_a = left_sums(spread_a), total(right_a[0], *came_a)
    one_a, left_b = fence((one_a, left_b))
    spread_b = over_y(left_b)
    one_x, two_x = swap(one_a, "xh"), swap(two_a, "xl")
    one_a, two_a = total(one_a, one_x), total(two_a, two_x)
    spread_b, one_a, two_a = fence((spread_b, one_a, two_a))

    rights_a = [two_a] + over_z([two_a] * Z)
    copies_a = left_copies(one_a)
    one_b, two_b = left_sums(spread_b), total(right_b[0], *came_b)
    one_b, copies_a = fence((one_b, copies_a))
    half_a = over_y(copies_a)
    one_x, two_x = swap(one_b, "xh"), swap(two_b, "xl")
    one_b, two_b = total(one_b, one_x), total(two_b, two_x)
    half_a, rights_a, one_b, two_b = fence((half_a, rights_a, one_b, two_b))

    rights_b = [two_b] + over_z([two_b] * Z)
    at = jnp.stack([core, z, row_first, col_first]).astype(jnp.int32)
    half_b = over_y(left_copies(one_b))
    product_a = product(A, None, at, sizes, half_a, swap(half_a, "core"), rights_a)
    half_b, rights_b, product_a = fence((half_b, rights_b, product_a))
    return product(B, order ** (-0.5), at, sizes, half_b, swap(half_b, "core"), rights_b, product_a)


def solution(mesh):
    split = Mesh(mesh.devices.reshape(Z, XL, Y, XH, CORE), ("z", "xl", "y", "xh", "core"))
    row, col = ("z", "xl"), ("y", "xh", "core")
    placed = (P(None, row, col), P(None, col, None), P(None, None, row), P(None, row, col), P())
    return jax.shard_map(
        on_device, mesh=split, in_specs=placed, out_specs=P(None, row, col), check_vma=False
    )
```

```python
import jax
import jax.numpy as jnp
from jax import lax
from jax.experimental import pallas as pl
from jax.experimental.pallas import tpu as pltpu
from jax.sharding import Mesh
from jax.sharding import PartitionSpec as P

WIDTH = 128
PART = 40
CHUNK = 4
Z, XL, Y, XH, CORE = 4, 2, 4, 2, 2
HALF = PART // CORE
ONE = HALF // Y
TWO = PART // Z
HBM = pl.BlockSpec(memory_space=pltpu.HBM)
ANY = pl.BlockSpec(memory_space=pl.ANY)
VMEM = pl.BlockSpec(memory_space=pltpu.VMEM)
SMEM = pl.BlockSpec(memory_space=pltpu.SMEM)
PARAMS = pltpu.CompilerParams(vmem_limit_bytes=60 * 2**20)


def packed(size_ref, lo, hi):
    first, chunk, plan = 0, 0, []
    for s in range(size_ref.shape[0]):
        blocks = lax.shift_right_logical(size_ref[s] + (WIDTH - 1), 7)
        begin, end = jnp.clip(lo - first, 0, blocks), jnp.clip(hi - first, 0, blocks)
        chunks = lax.shift_right_logical(end - begin + (CHUNK - 1), 2)
        plan.append((first, begin, end, chunk, chunks))
        first, chunk = first + blocks, chunk + chunks
    return plan, first


def most_chunks(slots, sectors):
    return (slots + sectors * (CHUNK - 1)) // CHUNK


def left_kernel(at_ref, size_ref, edge_ref, site_ref, *rest):
    outs, (out_buf, edge_buf, site_buf, edge_sem, site_sem, out_sem) = rest[: 2 * CORE], rest[2 * CORE :]
    core = at_ref[0]
    plan, used = packed(size_ref, 0, 2 * PART)
    def fetch(s, c):
        at = plan[s][3] + c
        columns = pl.ds(pl.multiple_of(c * (CHUNK * WIDTH), CHUNK * WIDTH), CHUNK * WIDTH)
        return pltpu.make_async_copy(site_ref.at[s, :, columns], site_buf.at[at], site_sem.at[at])

    edges = [pltpu.make_async_copy(edge_ref.at[s], edge_buf.at[s], edge_sem.at[s]) for s in range(len(plan))]
    for s in range(len(plan)):
        edges[s].start()

        @pl.loop(0, plan[s][4])
        def _(c):
            fetch(s, c).start()

    def send(piece):
        part, which = divmod(piece, CORE)
        k = jnp.where(core == which, 1, 0)
        for to in range(CORE):
            copy = pltpu.make_async_copy(
                out_buf.at[pl.ds(piece * HALF, HALF)], outs[part * CORE + to], out_sem.at[part * CORE + to]
            )
            pl.when(k == to)(copy.start)

    for s in range(len(plan)):
        first, _, blocks, chunk, chunks = plan[s]
        edges[s].wait()

        @pl.loop(0, chunks)
        def _(c):
            fetch(s, c).wait()
            term = jnp.dot(edge_buf[s], site_buf[chunk + c], preferred_element_type=jnp.float32)
            for k in range(CHUNK):
                out_buf[first + c * CHUNK + k] = term[:, k * WIDTH : (k + 1) * WIDTH].astype(out_buf.dtype)

        for piece in range(2 * CORE):
            edge = (piece + 1) * HALF
            pl.when((first < edge) & (first + blocks >= edge))(lambda piece=piece: send(piece))

    @pl.loop(used, 2 * PART)
    def _(q):
        out_buf[q] = jnp.zeros(out_buf.shape[1:], out_buf.dtype)

    for piece in range(2 * CORE):
        pl.when(used < (piece + 1) * HALF)(lambda piece=piece: send(piece))
    for k in range(2 * CORE):
        pltpu.make_async_copy(out_buf.at[pl.ds(0, HALF)], outs[k], out_sem.at[k]).wait()


def left_terms(core, sizes, edge, site):
    sectors, rows, depth = edge.shape
    most = most_chunks(2 * PART - 2, sectors)
    return pl.pallas_call(
        left_kernel,
        out_shape=[jax.ShapeDtypeStruct((HALF, rows, WIDTH), jnp.bfloat16)] * (2 * CORE),
        in_specs=[SMEM, SMEM, HBM, HBM],
        out_specs=[ANY] * (2 * CORE),
        scratch_shapes=[
            pltpu.VMEM((2 * PART + CHUNK, rows, WIDTH), jnp.bfloat16),
            pltpu.VMEM((sectors, rows, depth), jnp.bfloat16),
            pltpu.VMEM((most, depth, CHUNK * WIDTH), jnp.bfloat16),
            pltpu.SemaphoreType.DMA((sectors,)),
            pltpu.SemaphoreType.DMA((most,)),
            pltpu.SemaphoreType.DMA((2 * CORE,)),
        ],
        compiler_params=PARAMS,
        cost_estimate=pl.CostEstimate(
            flops=4 * PART * rows * depth * WIDTH, bytes_accessed=12 * 2**20, transcendentals=0
        ),
        name="left",
    )(core.reshape(1).astype(jnp.int32), sizes, edge, site)


def right_kernel(lo, at_ref, size_ref, edge_ref, site_ref, *rest):
    outs, (site_buf, edge_buf, term_buf, site_sem, edge_sem, out_sem) = rest[:Z], rest[Z:]
    z = at_ref[0]
    plan, used = packed(size_ref, lo, lo + PART)
    last = edge_ref.shape[1] // WIDTH - CHUNK

    def block_of(s, c):
        return jnp.minimum(plan[s][1] + c * CHUNK, last)

    def fetch(s, c):
        at = plan[s][3] + c
        rows = pl.ds(pl.multiple_of(block_of(s, c) * WIDTH, WIDTH), CHUNK * WIDTH)
        return pltpu.make_async_copy(edge_ref.at[s, rows, :], edge_buf.at[at], edge_sem.at[at])

    sites = [pltpu.make_async_copy(site_ref.at[s], site_buf.at[s], site_sem.at[s]) for s in range(len(plan))]
    for s in range(len(plan)):
        pl.when(plan[s][4] > 0)(sites[s].start)

        @pl.loop(0, plan[s][4])
        def _(c):
            fetch(s, c).start()

    def send(owner):
        piece = term_buf.at[pl.ds(owner * TWO + CHUNK, TWO)]
        for step in range(Z):
            copy = pltpu.make_async_copy(piece, outs[step], out_sem.at[step])
            pl.when(lax.rem(z + step, Z) == owner)(copy.start)

    for s in range(len(plan)):
        first, begin, end, chunk, chunks = plan[s]
        pl.when(chunks > 0)(sites[s].wait)

        @pl.loop(0, chunks)
        def _(c):
            fetch(s, c).wait()
            term = jnp.dot(edge_buf[chunk + c], site_buf[s], preferred_element_type=jnp.float32)
            q = first + block_of(s, c) - lo + CHUNK
            term_buf[pl.ds(q, CHUNK)] = term.astype(jnp.bfloat16).reshape(CHUNK, WIDTH, term.shape[1])

        for owner in range(Z):
            edge = lo + (owner + 1) * TWO
            pl.when((first + begin < edge) & (first + end >= edge))(lambda owner=owner: send(owner))

    for owner in range(Z):
        pl.when(used < lo + (owner + 1) * TWO)(lambda owner=owner: send(owner))
    for step in range(Z):
        pltpu.make_async_copy(term_buf.at[pl.ds(0, TWO)], outs[step], out_sem.at[step]).wait()


def right_terms(part, z, sizes, edge, site):
    sectors, depth, cols = site.shape
    most = most_chunks(PART, sectors)
    return pl.pallas_call(
        lambda *refs: right_kernel(part, *refs),
        out_shape=[jax.ShapeDtypeStruct((TWO, WIDTH, cols), jnp.bfloat16)] * Z,
        in_specs=[SMEM, SMEM, HBM, HBM],
        out_specs=[ANY] * Z,
        scratch_shapes=[
            pltpu.VMEM((sectors, depth, cols), jnp.bfloat16),
            pltpu.VMEM((most, CHUNK * WIDTH, depth), jnp.bfloat16),
            pltpu.VMEM((PART + 2 * CHUNK, WIDTH, cols), jnp.bfloat16),
            pltpu.SemaphoreType.DMA((sectors,)),
            pltpu.SemaphoreType.DMA((most,)),
            pltpu.SemaphoreType.DMA((Z,)),
        ],
        compiler_params=PARAMS,
        cost_estimate=pl.CostEstimate(
            flops=2 * PART * WIDTH * depth * cols, bytes_accessed=10 * 2**20, transcendentals=0
        ),
        name="right",
    )(z.reshape(1).astype(jnp.int32), sizes, edge, site)


def product_kernel(lo, scale, at_ref, size_ref, own_ref, other_ref, *rest):
    rights, rest = rest[:Z], rest[Z:]
    if scale is None:
        out_ref, one_buf, two_buf, sems = rest
    else:
        before_ref, out_ref, one_buf, two_buf, sems, before_buf = rest
    core, z, row_first, col_first = (at_ref[k] for k in range(4))
    plan, _ = packed(size_ref, lo, lo + PART)
    copies = [
        pltpu.make_async_copy(own_ref, one_buf.at[pl.ds(core * HALF, HALF)], sems.at[0]),
        pltpu.make_async_copy(other_ref, one_buf.at[pl.ds((1 - core) * HALF, HALF)], sems.at[1]),
    ]
    for step in range(Z):
        base = lax.rem(z + Z - step, Z) * TWO
        copies.append(pltpu.make_async_copy(rights[step], two_buf.at[pl.ds(base, TWO)], sems.at[2 + step]))
    if scale is not None:
        copies.append(pltpu.make_async_copy(before_ref, before_buf, sems.at[2 + Z]))
    for copy in copies:
        copy.start()
    for k in range(CHUNK):
        one_buf[PART + k] = jnp.zeros(one_buf.shape[1:], one_buf.dtype)
    for copy in copies:
        copy.wait()
    rows, cols = out_ref.shape[1:]
    deep = lax.broadcasted_iota(jnp.int32, (CHUNK * WIDTH, cols), 0)
    row = lax.broadcasted_iota(jnp.int32, (rows, cols), 0) + row_first
    col = lax.broadcasted_iota(jnp.int32, (rows, cols), 1) + col_first
    for s in range(len(plan)):
        first, begin, end, _, chunks = plan[s]
        size = size_ref[s]
        deep_end = jnp.minimum(size, end * WIDTH)

        def add(c, total):
            block = begin + c * CHUNK
            q = first + block - lo
            left = jnp.concatenate([one_buf[q + k] for k in range(CHUNK)], axis=1)
            right = two_buf[pl.ds(q, CHUNK)].reshape(CHUNK * WIDTH, cols)
            right = jnp.where(deep < deep_end - block * WIDTH, right, jnp.bfloat16(0.0))
            return total + jnp.dot(left, right, preferred_element_type=jnp.float32)

        start = jnp.zeros((rows, cols), jnp.float32) if scale is None else before_buf[s]
        total = lax.fori_loop(0, chunks, add, start)
        if scale is None:
            out_ref[s] = total
        else:
            live = (row < size) & (col < size)
            out_ref[s] = jnp.where(live, total * jnp.float32(scale), jnp.float32(0.0)).astype(out_ref.dtype)


def product(part, scale, at, sizes, own, other, rights, *before):
    rows, cols, sectors = own.shape[1], rights[0].shape[2], sizes.shape[0]
    shape = (sectors, rows, cols)
    end = bool(before)
    return pl.pallas_call(
        lambda *refs: product_kernel(part, scale, *refs),
        out_shape=jax.ShapeDtypeStruct(shape, jnp.bfloat16 if end else jnp.float32),
        in_specs=[SMEM, SMEM] + [ANY] * (2 + Z + end),
        out_specs=VMEM,
        scratch_shapes=[
            pltpu.VMEM((PART + CHUNK, rows, WIDTH), jnp.bfloat16),
            pltpu.VMEM((PART + CHUNK, WIDTH, cols), jnp.bfloat16),
            pltpu.SemaphoreType.DMA((2 + Z + end,)),
        ]
        + [pltpu.VMEM(shape, jnp.float32)] * end,
        compiler_params=pltpu.CompilerParams(vmem_limit_bytes=16 * 2**20),
        cost_estimate=pl.CostEstimate(
            flops=2 * PART * rows * WIDTH * cols, bytes_accessed=6 * 2**20, transcendentals=0
        ),
        name="product_end" if end else "product",
    )(at, sizes, own, other, *rights, *before)


def shift(array, axis, size, step):
    return lax.ppermute(array, axis, [(i, (i + step) % size) for i in range(size)])


def total(*terms):
    return sum(term.astype(jnp.float32) for term in terms).astype(jnp.bfloat16)


def over_z(arrays):
    return [shift(arrays[step], "z", Z, step) for step in range(1, Z)]


def over_y(array):
    return lax.all_to_all(array, "y", 0, 0, tiled=True)


def swap(array, axis):
    return shift(array, axis, 2, 1)


def on_device(edge_left, site_left, edge_right, site_right, sizes):
    order = site_left.shape[2]
    rows, cols = edge_left.shape[1], site_right.shape[2]
    z, xl, y, xh, core = (lax.axis_index(a) for a in ("z", "xl", "y", "xh", "core"))
    row_first = (z * XL + xl) * rows
    col_first = ((y * XH + xh) * CORE + core) * cols
    fence = lax.optimization_barrier
    A, B = 0, PART

    def left_sums(spread):
        return total(*spread.reshape((Y, ONE, rows, WIDTH)))

    def left_copies(own):
        return jnp.broadcast_to(own[None], (Y,) + own.shape).reshape(HALF, rows, WIDTH)

    goes_a, keeps_a, goes_b, keeps_b = left_terms(core, sizes, edge_left, site_left)
    came_a, came_b = swap(goes_a, "core"), swap(goes_b, "core")
    goes_a, right = fence((goes_a, (edge_right, site_right)))
    right_a = right_terms(A, z, sizes, *right)
    right_a, right, came_a = fence((right_a, right, came_a))
    left_a = total(keeps_a, came_a)

    came_a = over_z(right_a)
    left_a, right, keeps_b = fence((left_a, right, keeps_b))
    spread_a = over_y(left_a)
    right_b = right_terms(B, z, sizes, *right)
    left_b = total(keeps_b, came_b)
    spread_a, right_b, left_b = fence((spread_a, right_b, left_b))

    came_b = over_z(right_b)
    one_a, two_a = left_sums(spread_a), total(right_a[0], *came_a)
    one_a, left_b = fence((one_a, left_b))
    spread_b = over_y(left_b)
    one_x, two_x = swap(one_a, "xh"), swap(two_a, "xl")
    one_a, two_a = total(one_a, one_x), total(two_a, two_x)
    spread_b, one_a, two_a = fence((spread_b, one_a, two_a))

    rights_a = [two_a] + over_z([two_a] * Z)
    copies_a = left_copies(one_a)
    one_b, two_b = left_sums(spread_b), total(right_b[0], *came_b)
    one_b, copies_a = fence((one_b, copies_a))
    half_a = over_y(copies_a)
    one_x, two_x = swap(one_b, "xh"), swap(two_b, "xl")
    one_b, two_b = total(one_b, one_x), total(two_b, two_x)
    half_a, rights_a, one_b, two_b = fence((half_a, rights_a, one_b, two_b))

    rights_b = [two_b] + over_z([two_b] * Z)
    at = jnp.stack([core, z, row_first, col_first]).astype(jnp.int32)
    half_b = over_y(left_copies(one_b))
    product_a = product(A, None, at, sizes, half_a, swap(half_a, "core"), rights_a)
    half_b, rights_b, product_a = fence((half_b, rights_b, product_a))
    return product(B, order ** (-0.5), at, sizes, half_b, swap(half_b, "core"), rights_b, product_a)


def solution(mesh):
    split = Mesh(mesh.devices.reshape(Z, XL, Y, XH, CORE), ("z", "xl", "y", "xh", "core"))
    row, col = ("z", "xl"), ("y", "xh", "core")
    placed = (P(None, row, col), P(None, col, None), P(None, None, row), P(None, row, col), P())
    return jax.shard_map(
        on_device, mesh=split, in_specs=placed, out_specs=P(None, row, col), check_vma=False
    )
```

```python
import jax
import jax.numpy as jnp
from jax import lax
from jax.experimental import pallas as pl
from jax.experimental.pallas import tpu as pltpu
from jax.sharding import Mesh
from jax.sharding import PartitionSpec as P

WIDTH = 128
PART = 40
CHUNK = 4
Z, XL, Y, XH, CORE = 4, 2, 4, 2, 2
HALF = PART // CORE
ONE = HALF // Y
TWO = PART // Z
HBM = pl.BlockSpec(memory_space=pltpu.HBM)
ANY = pl.BlockSpec(memory_space=pl.ANY)
VMEM = pl.BlockSpec(memory_space=pltpu.VMEM)
SMEM = pl.BlockSpec(memory_space=pltpu.SMEM)
PARAMS = pltpu.CompilerParams(vmem_limit_bytes=60 * 2**20)


def packed(size_ref, lo, hi):
    first, chunk, plan = 0, 0, []
    for s in range(size_ref.shape[0]):
        blocks = lax.shift_right_logical(size_ref[s] + (WIDTH - 1), 7)
        begin, end = jnp.clip(lo - first, 0, blocks), jnp.clip(hi - first, 0, blocks)
        chunks = lax.shift_right_logical(end - begin + (CHUNK - 1), 2)
        plan.append((first, begin, end, chunk, chunks))
        first, chunk = first + blocks, chunk + chunks
    return plan, first


def most_chunks(slots, sectors):
    return (slots + sectors * (CHUNK - 1)) // CHUNK


def left_kernel(at_ref, size_ref, edge_ref, site_ref, *rest):
    outs, (out_buf, edge_buf, site_buf, edge_sem, site_sem, out_sem) = rest[: 2 * CORE], rest[2 * CORE :]
    core = at_ref[0]
    plan, used = packed(size_ref, 0, 2 * PART)
    def fetch(s, c):
        at = plan[s][3] + c
        columns = pl.ds(pl.multiple_of(c * (CHUNK * WIDTH), CHUNK * WIDTH), CHUNK * WIDTH)
        return pltpu.make_async_copy(site_ref.at[s, :, columns], site_buf.at[at], site_sem.at[at])

    edges = [pltpu.make_async_copy(edge_ref.at[s], edge_buf.at[s], edge_sem.at[s]) for s in range(len(plan))]
    for s in range(len(plan)):
        edges[s].start()

        @pl.loop(0, plan[s][4])
        def _(c):
            fetch(s, c).start()

    def send(piece):
        part, which = divmod(piece, CORE)
        k = jnp.where(core == which, 1, 0)
        for to in range(CORE):
            copy = pltpu.make_async_copy(
                out_buf.at[pl.ds(piece * HALF, HALF)], outs[part * CORE + to], out_sem.at[part * CORE + to]
            )
            pl.when(k == to)(copy.start)

    for s in range(len(plan)):
        first, _, blocks, chunk, chunks = plan[s]
        edges[s].wait()

        @pl.loop(0, chunks)
        def _(c):
            fetch(s, c).wait()
            term = jnp.dot(edge_buf[s], site_buf[chunk + c], preferred_element_type=jnp.float32)
            for k in range(CHUNK):
                out_buf[first + c * CHUNK + k] = term[:, k * WIDTH : (k + 1) * WIDTH].astype(out_buf.dtype)

        for piece in range(2 * CORE):
            edge = (piece + 1) * HALF
            pl.when((first < edge) & (first + blocks >= edge))(lambda piece=piece: send(piece))

    @pl.loop(used, 2 * PART)
    def _(q):
        out_buf[q] = jnp.zeros(out_buf.shape[1:], out_buf.dtype)

    for piece in range(2 * CORE):
        pl.when(used < (piece + 1) * HALF)(lambda piece=piece: send(piece))
    for k in range(2 * CORE):
        pltpu.make_async_copy(out_buf.at[pl.ds(0, HALF)], outs[k], out_sem.at[k]).wait()


def left_terms(core, sizes, edge, site):
    sectors, rows, depth = edge.shape
    most = most_chunks(2 * PART - 2, sectors)
    return pl.pallas_call(
        left_kernel,
        out_shape=[jax.ShapeDtypeStruct((HALF, rows, WIDTH), jnp.bfloat16)] * (2 * CORE),
        in_specs=[SMEM, SMEM, HBM, HBM],
        out_specs=[ANY] * (2 * CORE),
        scratch_shapes=[
            pltpu.VMEM((2 * PART + CHUNK, rows, WIDTH), jnp.bfloat16),
            pltpu.VMEM((sectors, rows, depth), jnp.bfloat16),
            pltpu.VMEM((most, depth, CHUNK * WIDTH), jnp.bfloat16),
            pltpu.SemaphoreType.DMA((sectors,)),
            pltpu.SemaphoreType.DMA((most,)),
            pltpu.SemaphoreType.DMA((2 * CORE,)),
        ],
        compiler_params=PARAMS,
        cost_estimate=pl.CostEstimate(
            flops=4 * PART * rows * depth * WIDTH, bytes_accessed=12 * 2**20, transcendentals=0
        ),
        name="left",
    )(core.reshape(1).astype(jnp.int32), sizes, edge, site)


def right_kernel(lo, at_ref, size_ref, edge_ref, site_ref, *rest):
    outs, (site_buf, edge_buf, term_buf, site_sem, edge_sem, out_sem) = rest[:Z], rest[Z:]
    z = at_ref[0]
    plan, used = packed(size_ref, lo, lo + PART)
    last = edge_ref.shape[1] // WIDTH - CHUNK

    def block_of(s, c):
        return jnp.minimum(plan[s][1] + c * CHUNK, last)

    def fetch(s, c):
        at = plan[s][3] + c
        rows = pl.ds(pl.multiple_of(block_of(s, c) * WIDTH, WIDTH), CHUNK * WIDTH)
        return pltpu.make_async_copy(edge_ref.at[s, rows, :], edge_buf.at[at], edge_sem.at[at])

    sites = [pltpu.make_async_copy(site_ref.at[s], site_buf.at[s], site_sem.at[s]) for s in range(len(plan))]
    for s in range(len(plan)):
        pl.when(plan[s][4] > 0)(sites[s].start)

        @pl.loop(0, plan[s][4])
        def _(c):
            fetch(s, c).start()

    def send(owner):
        piece = term_buf.at[pl.ds(owner * TWO + CHUNK, TWO)]
        for step in range(Z):
            copy = pltpu.make_async_copy(piece, outs[step], out_sem.at[step])
            pl.when(lax.rem(z + step, Z) == owner)(copy.start)

    for s in range(len(plan)):
        first, begin, end, chunk, chunks = plan[s]
        pl.when(chunks > 0)(sites[s].wait)

        @pl.loop(0, chunks)
        def _(c):
            fetch(s, c).wait()
            term = jnp.dot(edge_buf[chunk + c], site_buf[s], preferred_element_type=jnp.float32)
            q = first + block_of(s, c) - lo + CHUNK
            term_buf[pl.ds(q, CHUNK)] = term.astype(jnp.bfloat16).reshape(CHUNK, WIDTH, term.shape[1])

        for owner in range(Z):
            edge = lo + (owner + 1) * TWO
            pl.when((first + begin < edge) & (first + end >= edge))(lambda owner=owner: send(owner))

    for owner in range(Z):
        pl.when(used < lo + (owner + 1) * TWO)(lambda owner=owner: send(owner))
    for step in range(Z):
        pltpu.make_async_copy(term_buf.at[pl.ds(0, TWO)], outs[step], out_sem.at[step]).wait()


def right_terms(part, z, sizes, edge, site):
    sectors, depth, cols = site.shape
    most = most_chunks(PART, sectors)
    return pl.pallas_call(
        lambda *refs: right_kernel(part, *refs),
        out_shape=[jax.ShapeDtypeStruct((TWO, WIDTH, cols), jnp.bfloat16)] * Z,
        in_specs=[SMEM, SMEM, HBM, HBM],
        out_specs=[ANY] * Z,
        scratch_shapes=[
            pltpu.VMEM((sectors, depth, cols), jnp.bfloat16),
            pltpu.VMEM((most, CHUNK * WIDTH, depth), jnp.bfloat16),
            pltpu.VMEM((PART + 2 * CHUNK, WIDTH, cols), jnp.bfloat16),
            pltpu.SemaphoreType.DMA((sectors,)),
            pltpu.SemaphoreType.DMA((most,)),
            pltpu.SemaphoreType.DMA((Z,)),
        ],
        compiler_params=PARAMS,
        cost_estimate=pl.CostEstimate(
            flops=2 * PART * WIDTH * depth * cols, bytes_accessed=10 * 2**20, transcendentals=0
        ),
        name="right",
    )(z.reshape(1).astype(jnp.int32), sizes, edge, site)


def product_kernel(lo, scale, at_ref, size_ref, own_ref, other_ref, *rest):
    rights, rest = rest[:Z], rest[Z:]
    if scale is None:
        out_ref, one_buf, two_buf, sems = rest
    else:
        before_ref, out_ref, one_buf, two_buf, sems, before_buf = rest
    core, z, row_first, col_first = (at_ref[k] for k in range(4))
    plan, _ = packed(size_ref, lo, lo + PART)
    copies = [
        pltpu.make_async_copy(own_ref, one_buf.at[pl.ds(core * HALF, HALF)], sems.at[0]),
        pltpu.make_async_copy(other_ref, one_buf.at[pl.ds((1 - core) * HALF, HALF)], sems.at[1]),
    ]
    for step in range(Z):
        base = lax.rem(z + Z - step, Z) * TWO
        copies.append(pltpu.make_async_copy(rights[step], two_buf.at[pl.ds(base, TWO)], sems.at[2 + step]))
    if scale is not None:
        copies.append(pltpu.make_async_copy(before_ref, before_buf, sems.at[2 + Z]))
    for copy in copies:
        copy.start()
    for k in range(CHUNK):
        one_buf[PART + k] = jnp.zeros(one_buf.shape[1:], one_buf.dtype)
    for copy in copies:
        copy.wait()
    rows, cols = out_ref.shape[1:]
    deep = lax.broadcasted_iota(jnp.int32, (CHUNK * WIDTH, cols), 0)
    row = lax.broadcasted_iota(jnp.int32, (rows, cols), 0) + row_first
    col = lax.broadcasted_iota(jnp.int32, (rows, cols), 1) + col_first
    for s in range(len(plan)):
        first, begin, end, _, chunks = plan[s]
        size = size_ref[s]
        deep_end = jnp.minimum(size, end * WIDTH)

        def add(c, total):
            block = begin + c * CHUNK
            q = first + block - lo
            left = jnp.concatenate([one_buf[q + k] for k in range(CHUNK)], axis=1)
            right = two_buf[pl.ds(q, CHUNK)].reshape(CHUNK * WIDTH, cols)
            right = jnp.where(deep < deep_end - block * WIDTH, right, jnp.bfloat16(0.0))
            return total + jnp.dot(left, right, preferred_element_type=jnp.float32)

        start = jnp.zeros((rows, cols), jnp.float32) if scale is None else before_buf[s]
        total = lax.fori_loop(0, chunks, add, start)
        if scale is None:
            out_ref[s] = total
        else:
            live = (row < size) & (col < size)
            out_ref[s] = jnp.where(live, total * jnp.float32(scale), jnp.float32(0.0)).astype(out_ref.dtype)


def product(part, scale, at, sizes, own, other, rights, *before):
    rows, cols, sectors = own.shape[1], rights[0].shape[2], sizes.shape[0]
    shape = (sectors, rows, cols)
    end = bool(before)
    return pl.pallas_call(
        lambda *refs: product_kernel(part, scale, *refs),
        out_shape=jax.ShapeDtypeStruct(shape, jnp.bfloat16 if end else jnp.float32),
        in_specs=[SMEM, SMEM] + [ANY] * (2 + Z + end),
        out_specs=VMEM,
        scratch_shapes=[
            pltpu.VMEM((PART + CHUNK, rows, WIDTH), jnp.bfloat16),
            pltpu.VMEM((PART + CHUNK, WIDTH, cols), jnp.bfloat16),
            pltpu.SemaphoreType.DMA((2 + Z + end,)),
        ]
        + [pltpu.VMEM(shape, jnp.float32)] * end,
        compiler_params=pltpu.CompilerParams(vmem_limit_bytes=16 * 2**20),
        cost_estimate=pl.CostEstimate(
            flops=2 * PART * rows * WIDTH * cols, bytes_accessed=6 * 2**20, transcendentals=0
        ),
        name="product_end" if end else "product",
    )(at, sizes, own, other, *rights, *before)


def shift(array, axis, size, step):
    return lax.ppermute(array, axis, [(i, (i + step) % size) for i in range(size)])


def total(*terms):
    return sum(term.astype(jnp.float32) for term in terms).astype(jnp.bfloat16)


def over_z(arrays):
    return [shift(arrays[step], "z", Z, step) for step in range(1, Z)]


def over_y(array):
    return lax.all_to_all(array, "y", 0, 0, tiled=True)


def swap(array, axis):
    return shift(array, axis, 2, 1)


def on_device(edge_left, site_left, edge_right, site_right, sizes):
    order = site_left.shape[2]
    rows, cols = edge_left.shape[1], site_right.shape[2]
    z, xl, y, xh, core = (lax.axis_index(a) for a in ("z", "xl", "y", "xh", "core"))
    row_first = (z * XL + xl) * rows
    col_first = ((y * XH + xh) * CORE + core) * cols
    fence = lax.optimization_barrier
    A, B = 0, PART

    def left_sums(spread):
        return total(*spread.reshape((Y, ONE, rows, WIDTH)))

    def left_copies(own):
        return jnp.broadcast_to(own[None], (Y,) + own.shape).reshape(HALF, rows, WIDTH)

    goes_a, keeps_a, goes_b, keeps_b = left_terms(core, sizes, edge_left, site_left)
    came_a, came_b = swap(goes_a, "core"), swap(goes_b, "core")
    goes_a, right = fence((goes_a, (edge_right, site_right)))
    right_a = right_terms(A, z, sizes, *right)
    right_a, right, came_a = fence((right_a, right, came_a))
    left_a = total(keeps_a, came_a)

    came_a = over_z(right_a)
    left_a, right, keeps_b = fence((left_a, right, keeps_b))
    spread_a = over_y(left_a)
    right_b = right_terms(B, z, sizes, *right)
    left_b = total(keeps_b, came_b)
    spread_a, right_b, left_b = fence((spread_a, right_b, left_b))

    came_b = over_z(right_b)
    one_a, two_a = left_sums(spread_a), total(right_a[0], *came_a)
    one_a, left_b = fence((one_a, left_b))
    spread_b = over_y(left_b)
    one_x, two_x = swap(one_a, "xh"), swap(two_a, "xl")
    one_a, two_a = total(one_a, one_x), total(two_a, two_x)
    spread_b, one_a, two_a = fence((spread_b, one_a, two_a))

    rights_a = [two_a] + over_z([two_a] * Z)
    copies_a = left_copies(one_a)
    one_b, two_b = left_sums(spread_b), total(right_b[0], *came_b)
    one_b, copies_a = fence((one_b, copies_a))
    half_a = over_y(copies_a)
    one_x, two_x = swap(one_b, "xh"), swap(two_b, "xl")
    one_b, two_b = total(one_b, one_x), total(two_b, two_x)
    copies_b = left_copies(one_b)
    half_a, rights_a, copies_b, two_b = fence((half_a, rights_a, copies_b, two_b))

    rights_b = [two_b] + over_z([two_b] * Z)
    at = jnp.stack([core, z, row_first, col_first]).astype(jnp.int32)
    half_b = over_y(copies_b)
    product_a = product(A, None, at, sizes, half_a, swap(half_a, "core"), rights_a)
    half_b, rights_b, product_a = fence((half_b, rights_b, product_a))
    return product(B, order ** (-0.5), at, sizes, half_b, swap(half_b, "core"), rights_b, product_a)


def solution(mesh):
    split = Mesh(mesh.devices.reshape(Z, XL, Y, XH, CORE), ("z", "xl", "y", "xh", "core"))
    row, col = ("z", "xl"), ("y", "xh", "core")
    placed = (P(None, row, col), P(None, col, None), P(None, None, row), P(None, row, col), P())
    return jax.shard_map(
        on_device, mesh=split, in_specs=placed, out_specs=P(None, row, col), check_vma=False
    )
```

```python
import jax
import jax.numpy as jnp
from jax import lax
from jax.experimental import pallas as pl
from jax.experimental.pallas import tpu as pltpu
from jax.sharding import Mesh
from jax.sharding import PartitionSpec as P

WIDTH = 128
PART = 40
CHUNK = 4
DEEP = 8
Z, XL, Y, XH, CORE = 4, 2, 4, 2, 2
HALF = PART // CORE
ONE = HALF // Y
TWO = PART // Z
HBM = pl.BlockSpec(memory_space=pltpu.HBM)
ANY = pl.BlockSpec(memory_space=pl.ANY)
VMEM = pl.BlockSpec(memory_space=pltpu.VMEM)
SMEM = pl.BlockSpec(memory_space=pltpu.SMEM)
PARAMS = pltpu.CompilerParams(vmem_limit_bytes=60 * 2**20)


def packed(size_ref, lo, hi):
    first, chunk, plan = 0, 0, []
    for s in range(size_ref.shape[0]):
        blocks = lax.shift_right_logical(size_ref[s] + (WIDTH - 1), 7)
        begin, end = jnp.clip(lo - first, 0, blocks), jnp.clip(hi - first, 0, blocks)
        chunks = lax.shift_right_logical(end - begin + (CHUNK - 1), 2)
        plan.append((first, begin, end, chunk, chunks))
        first, chunk = first + blocks, chunk + chunks
    return plan, first


def most_chunks(slots, sectors):
    return (slots + sectors * (CHUNK - 1)) // CHUNK


def left_kernel(at_ref, size_ref, edge_ref, site_ref, *rest):
    outs, (out_buf, edge_buf, site_buf, edge_sem, site_sem, out_sem) = rest[: 2 * CORE], rest[2 * CORE :]
    core = at_ref[0]
    plan, used = packed(size_ref, 0, 2 * PART)
    def fetch(s, c):
        at = plan[s][3] + c
        columns = pl.ds(pl.multiple_of(c * (CHUNK * WIDTH), CHUNK * WIDTH), CHUNK * WIDTH)
        return pltpu.make_async_copy(site_ref.at[s, :, columns], site_buf.at[at], site_sem.at[at])

    edges = [pltpu.make_async_copy(edge_ref.at[s], edge_buf.at[s], edge_sem.at[s]) for s in range(len(plan))]
    for s in range(len(plan)):
        edges[s].start()

        @pl.loop(0, plan[s][4])
        def _(c):
            fetch(s, c).start()

    def send(piece):
        part, which = divmod(piece, CORE)
        k = jnp.where(core == which, 1, 0)
        for to in range(CORE):
            copy = pltpu.make_async_copy(
                out_buf.at[pl.ds(piece * HALF, HALF)], outs[part * CORE + to], out_sem.at[part * CORE + to]
            )
            pl.when(k == to)(copy.start)

    for s in range(len(plan)):
        first, _, blocks, chunk, chunks = plan[s]
        edges[s].wait()

        @pl.loop(0, chunks)
        def _(c):
            fetch(s, c).wait()
            term = jnp.dot(edge_buf[s], site_buf[chunk + c], preferred_element_type=jnp.float32)
            for k in range(CHUNK):
                out_buf[first + c * CHUNK + k] = term[:, k * WIDTH : (k + 1) * WIDTH].astype(out_buf.dtype)

        for piece in range(2 * CORE):
            edge = (piece + 1) * HALF
            pl.when((first < edge) & (first + blocks >= edge))(lambda piece=piece: send(piece))

    @pl.loop(used, 2 * PART)
    def _(q):
        out_buf[q] = jnp.zeros(out_buf.shape[1:], out_buf.dtype)

    for piece in range(2 * CORE):
        pl.when(used < (piece + 1) * HALF)(lambda piece=piece: send(piece))
    for k in range(2 * CORE):
        pltpu.make_async_copy(out_buf.at[pl.ds(0, HALF)], outs[k], out_sem.at[k]).wait()


def left_terms(core, sizes, edge, site):
    sectors, rows, depth = edge.shape
    most = most_chunks(2 * PART - 2, sectors)
    return pl.pallas_call(
        left_kernel,
        out_shape=[jax.ShapeDtypeStruct((HALF, rows, WIDTH), jnp.bfloat16)] * (2 * CORE),
        in_specs=[SMEM, SMEM, HBM, HBM],
        out_specs=[ANY] * (2 * CORE),
        scratch_shapes=[
            pltpu.VMEM((2 * PART + CHUNK, rows, WIDTH), jnp.bfloat16),
            pltpu.VMEM((sectors, rows, depth), jnp.bfloat16),
            pltpu.VMEM((most, depth, CHUNK * WIDTH), jnp.bfloat16),
            pltpu.SemaphoreType.DMA((sectors,)),
            pltpu.SemaphoreType.DMA((most,)),
            pltpu.SemaphoreType.DMA((2 * CORE,)),
        ],
        compiler_params=PARAMS,
        cost_estimate=pl.CostEstimate(
            flops=4 * PART * rows * depth * WIDTH, bytes_accessed=12 * 2**20, transcendentals=0
        ),
        name="left",
    )(core.reshape(1).astype(jnp.int32), sizes, edge, site)


def right_kernel(lo, at_ref, size_ref, edge_ref, site_ref, *rest):
    outs, (site_buf, edge_buf, term_buf, site_sem, edge_sem) = rest[:Z], rest[Z:]
    z = at_ref[0]
    plan, _ = packed(size_ref, lo, lo + PART)
    last = edge_ref.shape[1] // WIDTH - CHUNK

    def block_of(s, c):
        return jnp.minimum(plan[s][1] + c * CHUNK, last)

    def fetch(s, c):
        at = plan[s][3] + c
        rows = pl.ds(pl.multiple_of(block_of(s, c) * WIDTH, WIDTH), CHUNK * WIDTH)
        return pltpu.make_async_copy(edge_ref.at[s, rows, :], edge_buf.at[at], edge_sem.at[at])

    sites = [pltpu.make_async_copy(site_ref.at[s], site_buf.at[s], site_sem.at[s]) for s in range(len(plan))]
    for s in range(len(plan)):
        pl.when(plan[s][4] > 0)(sites[s].start)

        @pl.loop(0, plan[s][4])
        def _(c):
            fetch(s, c).start()

    for s in range(len(plan)):
        first, _, _, chunk, chunks = plan[s]
        pl.when(chunks > 0)(sites[s].wait)

        @pl.loop(0, chunks)
        def _(c):
            fetch(s, c).wait()
            term = jnp.dot(edge_buf[chunk + c], site_buf[s], preferred_element_type=jnp.float32)
            q = first + block_of(s, c) - lo + CHUNK
            term_buf[pl.ds(q, CHUNK)] = term.astype(jnp.bfloat16).reshape(CHUNK, WIDTH, term.shape[1])

    for step in range(Z):
        base = lax.rem(z + step, Z) * TWO + CHUNK
        for k in range(0, TWO, 2):
            outs[step][k : k + 2] = term_buf[pl.ds(base + k, 2)]


def right_terms(part, z, sizes, edge, site):
    sectors, depth, cols = site.shape
    most = most_chunks(PART, sectors)
    return pl.pallas_call(
        lambda *refs: right_kernel(part, *refs),
        out_shape=[jax.ShapeDtypeStruct((TWO, WIDTH, cols), jnp.bfloat16)] * Z,
        in_specs=[SMEM, SMEM, HBM, HBM],
        out_specs=[VMEM] * Z,
        scratch_shapes=[
            pltpu.VMEM((sectors, depth, cols), jnp.bfloat16),
            pltpu.VMEM((most, CHUNK * WIDTH, depth), jnp.bfloat16),
            pltpu.VMEM((PART + 2 * CHUNK, WIDTH, cols), jnp.bfloat16),
            pltpu.SemaphoreType.DMA((sectors,)),
            pltpu.SemaphoreType.DMA((most,)),
        ],
        compiler_params=PARAMS,
        cost_estimate=pl.CostEstimate(
            flops=2 * PART * WIDTH * depth * cols, bytes_accessed=10 * 2**20, transcendentals=0
        ),
        name="right",
    )(z.reshape(1).astype(jnp.int32), sizes, edge, site)


def product_kernel(lo, scale, at_ref, size_ref, own_ref, other_ref, *rest):
    rights, rest = rest[:Z], rest[Z:]
    if scale is None:
        out_ref, one_buf, two_buf, sems = rest
    else:
        before_ref, out_ref, one_buf, two_buf, sems, before_buf = rest
    core, z, row_first, col_first = (at_ref[k] for k in range(4))
    plan, _ = packed(size_ref, lo, lo + PART)
    copies = [
        pltpu.make_async_copy(own_ref, one_buf.at[pl.ds(core * HALF, HALF)], sems.at[0]),
        pltpu.make_async_copy(other_ref, one_buf.at[pl.ds((1 - core) * HALF, HALF)], sems.at[1]),
    ]
    for step in range(Z):
        base = lax.rem(z + Z - step, Z) * TWO
        copies.append(pltpu.make_async_copy(rights[step], two_buf.at[pl.ds(base, TWO)], sems.at[2 + step]))
    if scale is not None:
        copies.append(pltpu.make_async_copy(before_ref, before_buf, sems.at[2 + Z]))
    for copy in copies:
        copy.start()
    for k in range(DEEP):
        one_buf[PART + k] = jnp.zeros(one_buf.shape[1:], one_buf.dtype)
    for copy in copies:
        copy.wait()
    rows, cols = out_ref.shape[1:]
    deep = lax.broadcasted_iota(jnp.int32, (DEEP * WIDTH, cols), 0)
    row = lax.broadcasted_iota(jnp.int32, (rows, cols), 0) + row_first
    col = lax.broadcasted_iota(jnp.int32, (rows, cols), 1) + col_first
    for s in range(len(plan)):
        first, begin, end, _, _ = plan[s]
        chunks = lax.shift_right_logical(end - begin + (DEEP - 1), 3)
        size = size_ref[s]
        deep_end = jnp.minimum(size, end * WIDTH)

        def add(c, total):
            block = begin + c * DEEP
            q = first + block - lo
            left = jnp.concatenate([one_buf[q + k] for k in range(DEEP)], axis=1)
            right = two_buf[pl.ds(q, DEEP)].reshape(DEEP * WIDTH, cols)
            right = jnp.where(deep < deep_end - block * WIDTH, right, jnp.bfloat16(0.0))
            return total + jnp.dot(left, right, preferred_element_type=jnp.float32)

        start = jnp.zeros((rows, cols), jnp.float32) if scale is None else before_buf[s]
        total = lax.fori_loop(0, chunks, add, start)
        if scale is None:
            out_ref[s] = total
        else:
            live = (row < size) & (col < size)
            out_ref[s] = jnp.where(live, total * jnp.float32(scale), jnp.float32(0.0)).astype(out_ref.dtype)


def product(part, scale, at, sizes, own, other, rights, *before):
    rows, cols, sectors = own.shape[1], rights[0].shape[2], sizes.shape[0]
    shape = (sectors, rows, cols)
    end = bool(before)
    return pl.pallas_call(
        lambda *refs: product_kernel(part, scale, *refs),
        out_shape=jax.ShapeDtypeStruct(shape, jnp.bfloat16 if end else jnp.float32),
        in_specs=[SMEM, SMEM] + [ANY] * (2 + Z + end),
        out_specs=VMEM,
        scratch_shapes=[
            pltpu.VMEM((PART + DEEP, rows, WIDTH), jnp.bfloat16),
            pltpu.VMEM((PART + DEEP, WIDTH, cols), jnp.bfloat16),
            pltpu.SemaphoreType.DMA((2 + Z + end,)),
        ]
        + [pltpu.VMEM(shape, jnp.float32)] * end,
        compiler_params=pltpu.CompilerParams(vmem_limit_bytes=16 * 2**20),
        cost_estimate=pl.CostEstimate(
            flops=2 * PART * rows * WIDTH * cols, bytes_accessed=6 * 2**20, transcendentals=0
        ),
        name="product_end" if end else "product",
    )(at, sizes, own, other, *rights, *before)


def shift(array, axis, size, step):
    return lax.ppermute(array, axis, [(i, (i + step) % size) for i in range(size)])


def total(*terms):
    return sum(term.astype(jnp.float32) for term in terms).astype(jnp.bfloat16)


def over_z(arrays):
    return [shift(arrays[step], "z", Z, step) for step in range(1, Z)]


def over_y(array):
    return lax.all_to_all(array, "y", 0, 0, tiled=True)


def swap(array, axis):
    return shift(array, axis, 2, 1)


def on_device(edge_left, site_left, edge_right, site_right, sizes):
    order = site_left.shape[2]
    rows, cols = edge_left.shape[1], site_right.shape[2]
    z, xl, y, xh, core = (lax.axis_index(a) for a in ("z", "xl", "y", "xh", "core"))
    row_first = (z * XL + xl) * rows
    col_first = ((y * XH + xh) * CORE + core) * cols
    fence = lax.optimization_barrier
    A, B = 0, PART

    def left_sums(spread):
        return total(*spread.reshape((Y, ONE, rows, WIDTH)))

    def left_copies(own):
        return jnp.broadcast_to(own[None], (Y,) + own.shape).reshape(HALF, rows, WIDTH)

    goes_a, keeps_a, goes_b, keeps_b = left_terms(core, sizes, edge_left, site_left)
    came_a, came_b = swap(goes_a, "core"), swap(goes_b, "core")
    goes_a, right = fence((goes_a, (edge_right, site_right)))
    right_a = right_terms(A, z, sizes, *right)
    right_a, right, came_a = fence((right_a, right, came_a))
    left_a = total(keeps_a, came_a)

    came_a = over_z(right_a)
    left_a, right, keeps_b = fence((left_a, right, keeps_b))
    spread_a = over_y(left_a)
    right_b = right_terms(B, z, sizes, *right)
    left_b = total(keeps_b, came_b)
    spread_a, right_b, left_b = fence((spread_a, right_b, left_b))

    came_b = over_z(right_b)
    one_a, two_a = left_sums(spread_a), total(right_a[0], *came_a)
    one_a, left_b = fence((one_a, left_b))
    spread_b = over_y(left_b)
    one_x, two_x = swap(one_a, "xh"), swap(two_a, "xl")
    one_a, two_a = total(one_a, one_x), total(two_a, two_x)
    spread_b, one_a, two_a = fence((spread_b, one_a, two_a))

    rights_a = [two_a] + over_z([two_a] * Z)
    copies_a = left_copies(one_a)
    one_b, two_b = left_sums(spread_b), total(right_b[0], *came_b)
    one_b, copies_a = fence((one_b, copies_a))
    half_a = over_y(copies_a)
    one_x, two_x = swap(one_b, "xh"), swap(two_b, "xl")
    one_b, two_b = total(one_b, one_x), total(two_b, two_x)
    half_a, rights_a, one_b, two_b = fence((half_a, rights_a, one_b, two_b))

    rights_b = [two_b] + over_z([two_b] * Z)
    at = jnp.stack([core, z, row_first, col_first]).astype(jnp.int32)
    half_b = over_y(left_copies(one_b))
    product_a = product(A, None, at, sizes, half_a, swap(half_a, "core"), rights_a)
    half_b, rights_b, product_a = fence((half_b, rights_b, product_a))
    return product(B, order ** (-0.5), at, sizes, half_b, swap(half_b, "core"), rights_b, product_a)


def solution(mesh):
    split = Mesh(mesh.devices.reshape(Z, XL, Y, XH, CORE), ("z", "xl", "y", "xh", "core"))
    row, col = ("z", "xl"), ("y", "xh", "core")
    placed = (P(None, row, col), P(None, col, None), P(None, None, row), P(None, row, col), P())
    return jax.shard_map(
        on_device, mesh=split, in_specs=placed, out_specs=P(None, row, col), check_vma=False
    )
```
